128 devices in a mesh: col: 4 (over x_hi, core), af: 32 (over z, x_lo, y).
Axes of the slice: x: 4 (x_hi: 2, x_lo: 2; x = x_hi * 2 + x_lo), y: 4, z: 4, core: 2. Of those that a mesh axis runs over, the one named last changes fastest.
Arguments:
- coarse_state: float32 [3, 8, 512, 1024], P(None, None, 'af', 'col'), may hold values from 0.1 to 2
- coarse_kappa: float32 [8, 512, 1024], P(None, 'af', 'col'), may hold values from 0.25 to 1
- coarse_rate: float32 [8, 512, 1024], P(None, 'af', 'col'), may hold values from 0.5 to 6
- fine_state: float32 [512, 3, 32, 1024], P(('col', 'af')), may hold values from 0.1 to 2
- fine_kappa: float32 [512, 32, 1024], P(('col', 'af')), may hold values from 0.25 to 1
- fine_rate: float32 [512, 32, 1024], P(('col', 'af')), may hold values from 0.5 to 6
- boxes: int32 [512, 2], replicated, may hold values from 0 to 127, as said below
- cover: int32 [64, 128], replicated, may hold values from -1 to 511, as said below
Outputs:
- coarse_out: float32 [3, 8, 512, 1024], P(None, None, 'af', 'col')
- fine_out: float32 [512, 3, 32, 1024], P(('col', 'af'))
The draws below stay inside these ranges and needn't reach their ends.
Inputs may be any that keep to these rules, and one draw needn't show every extreme that they name: `boxes`: A patch's block spans all 8 planes; it lies in the 32 block rows of one col index, never in the first or last of them nor in the slab's first or last block column, and no two patches share a face. The patches whose blocks lie in one col index's rows are the rows of the fine arrays held by that col index, in no particular order. The 2 block columns of one af index hold at most 10 patches, and in every col index some af index holds exactly that many. cover[bx, by] is the patch whose block is (bx, by), or -1 where none is; it agrees with boxes, and every patch appears once.
All inputs are finite; a program needn't handle non-finite values.
Results may differ from the reference program's by a relative error of at most 0.0003.
Values sent between devices are 32-bit elements; how exact they have to be, the bound alone decides.
A program may use at most 192 MiB of HBM per device.

```python
import math
import jax
import jax.numpy as jnp
from jax import lax

NZC = 8
RATIO = 4
BLK = 8
CXB = 2
CYB = 32
SLOT_DEV = 4
MOST_OWN = 10
NBX = 64
NBY = 128
NXC = 512
NYC = 1024
PATCHES = 512
FZ = 32
FXY = 1024
N_COL = 4
N_AF = 32


def owner_counts(key):
    others = N_AF - 1
    share_total = N_AF * SLOT_DEV - MOST_OWN
    base_count = share_total // others
    leftover = share_total - base_count * others
    key_star, key_extra = jax.random.split(key, 2)
    busiest = jax.random.randint(key_star, (), 1, N_AF - 1)
    ranking = jax.random.permutation(key_extra, others)
    counts = base_count + (ranking < leftover).astype(jnp.int32)
    owners = jnp.arange(N_AF, dtype=jnp.int32)
    shifted = jnp.clip(owners - (owners > busiest).astype(jnp.int32), 0, others - 1)
    return jnp.where(owners == busiest, MOST_OWN, counts[shifted]).astype(jnp.int32)


def region_pick(key, col_id, owner_id, wanted):
    cell_count = CXB * CYB
    region_key = jax.random.fold_in(jax.random.fold_in(key, col_id + 1000), owner_id)
    priority = jax.random.permutation(region_key, cell_count).reshape(CXB, CYB)
    global_x = owner_id * CXB + jnp.arange(CXB, dtype=jnp.int32)[:, None]
    local_y = jnp.arange(CYB, dtype=jnp.int32)[None, :]
    global_y = col_id * CYB + local_y
    eligible = ((global_x + global_y) % 2 == 0) & (global_x >= 1) & (global_x <= NBX - 2) & (local_y >= 1) & (local_y <= CYB - 2)
    scores = jnp.where(eligible, priority, priority + cell_count).reshape(-1)
    ranks = jnp.argsort(jnp.argsort(scores, stable=True), stable=True)
    return (ranks < wanted).reshape(CXB, CYB)


def relabel(key, col_id, grid_row):
    group_size = N_AF * SLOT_DEV
    ranks = jnp.clip(jnp.cumsum(grid_row).astype(jnp.int32) - 1, 0, group_size - 1)
    shuffled = jax.random.permutation(jax.random.fold_in(key, col_id + 5000), group_size).astype(jnp.int32)
    first_owner = jnp.argmax(grid_row).astype(jnp.int32) // CYB // CXB
    target = ((first_owner + N_AF // 2) % N_AF * SLOT_DEV).astype(jnp.int32)
    first_value = shuffled[0]
    shuffled = jnp.where(shuffled == target, first_value, shuffled)
    shuffled = shuffled.at[0].set(target)
    labels = shuffled[ranks] + col_id * group_size
    return jnp.where(grid_row > 0, labels, -1).astype(jnp.int32)


def patch_layout(key):
    base_key = jax.random.fold_in(key, 77)
    col_ids = jnp.arange(N_COL, dtype=jnp.int32)
    counts = jax.vmap(lambda col_id: owner_counts(jax.random.fold_in(base_key, col_id)))(col_ids)
    owner_ids = jnp.arange(N_AF, dtype=jnp.int32)
    chosen = jax.vmap(lambda col_id, want_row: jax.vmap(lambda owner_id, wanted: region_pick(base_key, col_id, owner_id, wanted))(owner_ids, want_row))(col_ids, counts)
    flat_grid = chosen.reshape(N_COL, NBX * CYB).astype(jnp.int32)
    cover_cols = jax.vmap(lambda col_id, grid_row: relabel(base_key, col_id, grid_row))(col_ids, flat_grid).reshape(N_COL, NBX, CYB)
    cover = cover_cols.transpose(1, 0, 2).reshape(NBX, NBY).astype(jnp.int32)
    grid_x = jnp.broadcast_to(jnp.arange(NBX, dtype=jnp.int32)[:, None], (NBX, NBY))
    grid_y = jnp.broadcast_to(jnp.arange(NBY, dtype=jnp.int32)[None, :], (NBX, NBY))
    target = jnp.where(cover >= 0, cover, PATCHES).reshape(-1)
    boxes = jnp.zeros((PATCHES, 2), jnp.int32)
    boxes = boxes.at[target, 0].set(grid_x.reshape(-1), mode='drop')
    boxes = boxes.at[target, 1].set(grid_y.reshape(-1), mode='drop')
    return (boxes, cover)


def draw_boxes(key, part):
    return patch_layout(key)[0]


def draw_cover(key, part):
    return patch_layout(key)[1]


def block_levels(own_key, dims, cuts, smallest, largest):
    def one(axis_at, blocks):
        steps = jax.random.uniform(jax.random.fold_in(jax.random.fold_in(own_key, 6), axis_at), (blocks,), jnp.float32, smallest / len(cuts), largest / len(cuts))
        return jnp.repeat(jnp.exp(steps), dims[axis_at] // blocks).reshape((-1,) + (1,) * (len(dims) - axis_at - 1))

    gain = one(*cuts[0])
    for cut in cuts[1:]:
        gain = gain * one(*cut)
    return gain


def setup_inputs(seed: int = 0) -> dict:
    splits = jax.random.split(jax.random.key(seed), 9)
    coarse_state = jnp.clip(0.1 + 1.9 * jax.random.uniform(splits[0], (3, NZC, NXC, NYC), jnp.float32) ** block_levels(splits[0], (3, NZC, NXC, NYC), ((2, 32), (3, 4)), -0.2, 0.2), 0.1, 2.0)
    coarse_kappa = jnp.clip(jnp.exp(math.log(1.0) - 1.3862944 * jax.random.uniform(splits[1], (NZC, NXC, NYC), jnp.float32) ** block_levels(splits[1], (NZC, NXC, NYC), ((1, 32), (2, 4)), -0.2, 0.2)), 0.25, 1.0)
    coarse_rate = jnp.clip(jnp.exp(math.log(6.0) - 2.4849066 * jax.random.uniform(splits[2], (NZC, NXC, NYC), jnp.float32) ** block_levels(splits[2], (NZC, NXC, NYC), ((1, 32), (2, 4)), -0.2, 0.2)), 0.5, 6.0)
    fine_state = jnp.clip(0.1 + 1.9 * jax.random.uniform(splits[3], (PATCHES, 3, FZ, FXY), jnp.float32) ** block_levels(splits[3], (PATCHES, 3, FZ, FXY), ((0, 128),), -0.2, 0.2), 0.1, 2.0)
    fine_kappa = jnp.clip(jnp.exp(math.log(1.0) - 1.3862944 * jax.random.uniform(splits[4], (PATCHES, FZ, FXY), jnp.float32) ** block_levels(splits[4], (PATCHES, FZ, FXY), ((0, 128),), -0.2, 0.2)), 0.25, 1.0)
    fine_rate = jnp.clip(jnp.exp(math.log(6.0) - 2.4849066 * jax.random.uniform(splits[5], (PATCHES, FZ, FXY), jnp.float32) ** block_levels(splits[5], (PATCHES, FZ, FXY), ((0, 128),), -0.2, 0.2)), 0.5, 6.0)
    boxes = draw_boxes(jax.random.fold_in(splits[8], 71), 0)
    cover = draw_cover(jax.random.fold_in(splits[8], 71), 0)
    return {"coarse_state": coarse_state, "coarse_kappa": coarse_kappa, "coarse_rate": coarse_rate, "fine_state": fine_state, "fine_kappa": fine_kappa, "fine_rate": fine_rate, "boxes": boxes, "cover": cover}


DT_COARSE = 1.0 / 28.0
DIFFUSE = (1.0, 0.7, 0.45)
NEIGHBOURS = ((1, 0, 0), (-1, 0, 0), (0, 1, 0), (0, -1, 0), (0, 0, 1), (0, 0, -1))


def harmonic(first, second):
    summed = first + second
    positive = summed > 0.0
    return jnp.where(positive, 2.0 * first * second / jnp.where(positive, summed, 1.0), 0.0)


def combine(center, conduct, neighbour_list, reaction, inv_square, step_size):
    summed = jnp.zeros_like(center)
    for values, coeffs in neighbour_list:
        summed = summed + harmonic(conduct, coeffs) * (values - center)
    spread = jnp.stack([DIFFUSE[0] * summed[0], DIFFUSE[1] * summed[1], DIFFUSE[2] * summed[2]]) * inv_square
    forward = reaction * (center[0] * center[1] - center[2])
    change = spread + jnp.stack([-forward, -forward, forward])
    return center + step_size * change


def window(values, step_z, step_x, step_y):
    depth_len = values.shape[-3] - 2
    across = values.shape[-2] - 2
    along_len = values.shape[-1] - 2
    return values[..., 1 + step_z:1 + step_z + depth_len, 1 + step_x:1 + step_x + across, 1 + step_y:1 + step_y + along_len]


def coarse_advance(padded_xy, conduct_xy, reaction):
    padded = jnp.pad(padded_xy, ((0, 0), (1, 1), (0, 0), (0, 0)))
    conduct = jnp.pad(conduct_xy, ((1, 1), (0, 0), (0, 0)))
    neighbour_list = [(window(padded, offsets[0], offsets[1], offsets[2]), window(conduct, offsets[0], offsets[1], offsets[2])) for offsets in NEIGHBOURS]
    return combine(window(padded, 0, 0, 0), window(conduct, 0, 0, 0), neighbour_list, reaction, 1.0, DT_COARSE)


def upsample(strips):
    return jnp.repeat(jnp.repeat(strips, RATIO, axis=-2), RATIO, axis=-1)


def patch_step(fields, conduct, reaction, strips):
    ghosts = upsample(strips)
    edge_len = ghosts.shape[-1]
    position = lax.broadcasted_iota(jnp.int32, (1, edge_len * edge_len), 1)
    column = position % edge_len
    row_pos = position // edge_len
    zero_fields = jnp.zeros_like(fields[:, :1])
    zero_conduct = jnp.zeros_like(conduct[:1])
    upward = (jnp.concatenate([fields[:, 1:], zero_fields], axis=1), jnp.concatenate([conduct[1:], zero_conduct], axis=0))
    downward = (jnp.concatenate([zero_fields, fields[:, :-1]], axis=1), jnp.concatenate([zero_conduct, conduct[:-1]], axis=0))
    last_row = row_pos == edge_len - 1
    first_row = row_pos == 0
    last_col = column == edge_len - 1
    first_col = column == 0
    next_x = (jnp.where(last_row, jnp.tile(ghosts[1], (1, 1, edge_len)), jnp.roll(fields, -edge_len, axis=-1)), jnp.where(last_row, conduct, jnp.roll(conduct, -edge_len, axis=-1)))
    prev_x = (jnp.where(first_row, jnp.tile(ghosts[0], (1, 1, edge_len)), jnp.roll(fields, edge_len, axis=-1)), jnp.where(first_row, conduct, jnp.roll(conduct, edge_len, axis=-1)))
    next_y = (jnp.where(last_col, jnp.repeat(ghosts[3], edge_len, axis=-1), jnp.roll(fields, -1, axis=-1)), jnp.where(last_col, conduct, jnp.roll(conduct, -1, axis=-1)))
    prev_y = (jnp.where(first_col, jnp.repeat(ghosts[2], edge_len, axis=-1), jnp.roll(fields, 1, axis=-1)), jnp.where(first_col, conduct, jnp.roll(conduct, 1, axis=-1)))
    return combine(fields, conduct, [upward, downward, next_x, prev_x, next_y, prev_y], reaction, float(RATIO * RATIO), DT_COARSE / RATIO)


def restrict(fields):
    shaped = fields.reshape(3, NZC, RATIO, BLK, RATIO, BLK, RATIO)
    return jnp.mean(shaped, axis=(2, 4, 6)).reshape(-1)


def patch_rims(coarse, block_xy):
    anchor = jnp.zeros((), jnp.int32)
    start_x = (block_xy[0] * BLK).astype(jnp.int32)
    start_y = (block_xy[1] * BLK).astype(jnp.int32)
    lower_x = lax.dynamic_slice(coarse, (anchor, anchor, start_x - 1, start_y), (3, NZC, 1, BLK))[:, :, 0, :]
    upper_x = lax.dynamic_slice(coarse, (anchor, anchor, start_x + BLK, start_y), (3, NZC, 1, BLK))[:, :, 0, :]
    lower_y = lax.dynamic_slice(coarse, (anchor, anchor, start_x, start_y - 1), (3, NZC, BLK, 1))[:, :, :, 0]
    upper_y = lax.dynamic_slice(coarse, (anchor, anchor, start_x, start_y + BLK), (3, NZC, BLK, 1))[:, :, :, 0]
    return jnp.stack([lower_x, upper_x, lower_y, upper_y])


def reference(coarse_state, coarse_kappa, coarse_rate, fine_state, fine_kappa, fine_rate, boxes, cover):
    padded = jnp.pad(coarse_state, ((0, 0), (0, 0), (1, 1), (1, 1)))
    conduct = jnp.pad(coarse_kappa, ((0, 0), (1, 1), (1, 1)))
    coarse_new = coarse_advance(padded, conduct, coarse_rate)

    def one_patch(patch_items):
        fields, patch_kappa, patch_rate, block_xy = patch_items
        earlier = patch_rims(coarse_state, block_xy)
        updated = patch_rims(coarse_new, block_xy)
        for substep in range(RATIO):
            fraction = substep / RATIO
            strips = earlier + fraction * (updated - earlier)
            fields = patch_step(fields, patch_kappa, patch_rate, strips)
        return fields, restrict(fields)

    group_count = PATCHES // 32
    batched = jax.vmap(one_patch)
    stacked = (fine_state.reshape(group_count, 32, 3, FZ, FXY), fine_kappa.reshape(group_count, 32, FZ, FXY), fine_rate.reshape(group_count, 32, FZ, FXY), boxes.reshape(group_count, 32, 2))
    fine_out, averages = lax.map(batched, stacked)
    fine_out = fine_out.reshape(PATCHES, 3, FZ, FXY)
    averages = averages.reshape(PATCHES, -1)
    picked = averages[jnp.maximum(cover, 0)]
    picked = picked.reshape(NBX, NBY, 3, NZC, BLK, BLK).transpose(2, 3, 0, 4, 1, 5).reshape(3, NZC, NXC, NYC)
    covered = jnp.repeat(jnp.repeat(cover >= 0, BLK, axis=0), BLK, axis=1)
    coarse_out = jnp.where(covered[None, None], picked, coarse_new)
    return coarse_out, fine_out
```

```python
import jax
import jax.numpy as jnp
from jax import lax
from jax.experimental import pallas as pl
from jax.experimental.pallas import tpu as pltpu
from jax.sharding import PartitionSpec as P

NZC = 8
RATIO = 4
BLK = 8
SLOT_DEV = 4
FZ = 32
FXY = 1024
TILES = FXY // 128
FINE_DT = 1.0 / 112.0
FINE_SCALE = 16.0 / 112.0


DT_COARSE = 1.0 / 28.0
DIFFUSE = (1.0, 0.7, 0.45)
NEIGHBOURS = ((1, 0, 0), (-1, 0, 0), (0, 1, 0), (0, -1, 0), (0, 0, 1), (0, 0, -1))


def with_halo(cells, sides, width):
    for axis, dim in sides:
        count = lax.axis_size(axis)
        ends = count - 1
        head = lax.slice_in_dim(cells, 0, width, axis=dim)
        tail = lax.slice_in_dim(cells, cells.shape[dim] - width, cells.shape[dim], axis=dim)
        cells = jnp.concatenate(
            [
                lax.ppermute(tail, axis, [(i, (i + 1) % count) for i in range(ends)]),
                cells,
                lax.ppermute(head, axis, [((i + 1) % count, i) for i in range(ends)]),
            ],
            axis=dim,
        )
    return cells


def harmonic(first, second):
    summed = first + second
    positive = summed > 0.0
    return jnp.where(positive, 2.0 * first * second / jnp.where(positive, summed, 1.0), 0.0)


def combine(center, conduct, neighbour_list, reaction, inv_square, step_size):
    summed = jnp.zeros_like(center)
    for values, coeffs in neighbour_list:
        summed = summed + harmonic(conduct, coeffs) * (values - center)
    spread = (
        jnp.stack([DIFFUSE[0] * summed[0], DIFFUSE[1] * summed[1], DIFFUSE[2] * summed[2]])
        * inv_square
    )
    forward = reaction * (center[0] * center[1] - center[2])
    change = spread + jnp.stack([-forward, -forward, forward])
    return center + step_size * change


def window(values, step_z, step_x, step_y):
    depth_len = values.shape[-3] - 2
    across = values.shape[-2] - 2
    along_len = values.shape[-1] - 2
    return values[
        ...,
        1 + step_z : 1 + step_z + depth_len,
        1 + step_x : 1 + step_x + across,
        1 + step_y : 1 + step_y + along_len,
    ]


def coarse_advance(padded_xy, conduct_xy, reaction):
    padded = jnp.pad(padded_xy, ((0, 0), (1, 1), (0, 0), (0, 0)))
    conduct = jnp.pad(conduct_xy, ((1, 1), (0, 0), (0, 0)))
    neighbour_list = [
        (
            window(padded, offsets[0], offsets[1], offsets[2]),
            window(conduct, offsets[0], offsets[1], offsets[2]),
        )
        for offsets in NEIGHBOURS
    ]
    return combine(
        window(padded, 0, 0, 0), window(conduct, 0, 0, 0), neighbour_list, reaction, 1.0, DT_COARSE
    )


def lanes(shape=(8, 128)):
    return lax.broadcasted_iota(jnp.int32, shape, 1)


def rot(x, shift):
    return pltpu.roll(x, shift % x.shape[1], 1)


def face(p, q):
    both = p + q
    return (2.0 * FINE_SCALE) * p * q / both


def load_patch(fs, fk, fr, p, stage_u, stage_k, stage_r, sem):
    copies = []
    for t in range(TILES):
        cut = pl.ds(t * 128, 128)
        copies.append(pltpu.make_async_copy(fs.at[p, :, :, cut], stage_u.at[p, :, t], sem.at[p]))
        copies.append(pltpu.make_async_copy(fk.at[p, :, cut], stage_k.at[p, t], sem.at[p]))
        copies.append(pltpu.make_async_copy(fr.at[p, :, cut], stage_r.at[p, t], sem.at[p]))
    return copies


def patch_setup(p, stage_u, stage_k, stage_r, U, HZ, HX, HY, HM, HT, KY, KX, RT):
    lane = lanes()
    col = lane % 32
    sub = lax.broadcasted_iota(jnp.int32, (8, 128), 0)
    zero = jnp.zeros((8, 128), jnp.float32)
    for t in range(TILES):
        cut = pl.ds(t * 128, 128)
        for s in range(3):
            for j in range(RATIO):
                U[0, s, j + 1, :, cut] = stage_u[p, s, t, pl.ds(j, 8, stride=4), :]
    for j in range(RATIO):
        cond = [stage_k[p, t, pl.ds(j, 8, stride=4), :] for t in range(TILES)]
        for t in range(TILES):
            cut = pl.ds(t * 128, 128)
            k = cond[t]
            RT[j, :, cut] = stage_r[p, t, pl.ds(j, 8, stride=4), :] * FINE_DT
            if j < RATIO - 1:
                HZ[j + 1, :, cut] = face(k, stage_k[p, t, pl.ds(j + 1, 8, stride=4), :])
            else:
                above = stage_k[p, t, pl.ds(0, 8, stride=4), :]
                up = jnp.where(sub == 7, 0.0, face(k, pltpu.roll(above, 7, 0)))
                HZ[RATIO, :, cut] = up
                HZ[0, :, cut] = jnp.where(sub == 0, 0.0, pltpu.roll(up, 1, 0))
            here = rot(k, -32)
            if t < TILES - 1:
                ahead = jnp.where(lane < 96, here, rot(cond[t + 1], -32))
                hx = face(k, ahead)
            else:
                hx = jnp.where(lane < 96, face(k, here), 0.0)
            HX[j, 0, :, cut] = hx
            hy = jnp.where(col == 31, 0.0, face(k, rot(k, -1)))
            HY[j, 0, :, cut] = hy
            HY[j, 1, :, cut] = jnp.where(col == 0, 0.0, rot(hy, 1))
            KY[j, :, cut] = jnp.where((col == 0) | (col == 31), k * FINE_SCALE, 0.0)
        KX[j, 0] = jnp.where(lane < 32, cond[0] * FINE_SCALE, 0.0)
        KX[j, 1] = jnp.where(lane >= 96, cond[TILES - 1] * FINE_SCALE, 0.0)
    for j in range(RATIO):
        last = zero
        for t in range(TILES):
            cut = pl.ds(t * 128, 128)
            moved = rot(HX[j, 0, :, cut], 32)
            behind = jnp.where(lane >= 32, moved, last)
            last = moved
            HX[j, 1, :, cut] = behind
            total = (HX[j, 0, :, cut] + behind) + (HY[j, 0, :, cut] + HY[j, 1, :, cut])
            total = total + (HZ[j, :, cut] + HZ[j + 1, :, cut]) + KY[j, :, cut]
            if t == 0:
                total = total + KX[j, 0]
            if t == TILES - 1:
                total = total + KX[j, 1]
            HT[j, :, cut] = total


def ghost_setup(old, new, GH):
    lane = lanes()
    delta = (new - old) * (1.0 / RATIO)
    for s in range(3):
        for t in range(TILES):
            pick = s * 32 + 16 + t + jnp.where(lane % 32 == 31, 8, 0)
            GH[0, s, t] = jnp.take_along_axis(old, pick, axis=1)
            GH[1, s, t] = jnp.take_along_axis(delta, pick, axis=1)
        pick = s * 32 + jnp.where(lane < 64, lane // 4, (lane - 96) // 4 + 8) % 16
        GH[0, s, TILES] = jnp.take_along_axis(old, pick, axis=1)
        GH[1, s, TILES] = jnp.take_along_axis(delta, pick, axis=1)


def substep(now, U, HZ, HX, HY, HT, KY, KX, RT, GH):
    lane = lanes()
    later = 1 - now
    for s in range(3):
        U[now, s, 0] = pltpu.roll(U[now, s, RATIO], 1, 0)
        U[now, s, RATIO + 1] = pltpu.roll(U[now, s, 1], 7, 0)

    def plane(j, carry):
        for t in range(TILES):
            cut = pl.ds(t * 128, 128)
            hzu, hzd = HZ[j + 1, :, cut], HZ[j, :, cut]
            hxu, hxd = HX[j, 0, :, cut], HX[j, 1, :, cut]
            hyu, hyd = HY[j, 0, :, cut], HY[j, 1, :, cut]
            ht, ky, rt = HT[j, :, cut], KY[j, :, cut], RT[j, :, cut]
            us = [U[now, s, j + 1, :, cut] for s in range(3)]
            react = rt * (us[0] * us[1] - us[2])
            for s in range(3):
                u = us[s]
                up = rot(u, -32)
                if t < TILES - 1:
                    up = jnp.where(lane < 96, up, rot(U[now, s, j + 1, :, pl.ds(t * 128 + 128, 128)], -32))
                down = rot(u, 32)
                if t > 0:
                    down = jnp.where(lane >= 32, down, rot(U[now, s, j + 1, :, pl.ds(t * 128 - 128, 128)], 32))
                flow = (hzu * U[now, s, j + 2, :, cut] + hzd * U[now, s, j, :, cut]) + (hxu * up + hxd * down)
                flow = flow + (hyu * rot(u, -1) + hyd * rot(u, 1)) + (ky * GH[0, s, t] - ht * u)
                if t == 0:
                    flow = flow + KX[j, 0] * GH[0, s, TILES]
                if t == TILES - 1:
                    flow = flow + KX[j, 1] * GH[0, s, TILES]
                if s > 0:
                    flow = DIFFUSE[s] * flow
                U[later, s, j + 1, :, cut] = u + (flow - react if s < 2 else flow + react)
        return carry

    lax.fori_loop(0, RATIO, plane, 0)
    GH[0] = GH[0] + GH[1]


def patch_average(final, U):
    rows = lax.broadcasted_iota(jnp.int32, (FXY, 128), 0)
    cols = lax.broadcasted_iota(jnp.int32, (FXY, 128), 1)
    weights = jnp.where(cols == (rows // 128) * 8 + (rows % 32) // 4, 1.0 / 64.0, 0.0).astype(jnp.bfloat16)
    sums = [
        (U[final, s, 1] + U[final, s, 2]) + (U[final, s, 3] + U[final, s, 4]) for s in range(3)
    ]
    value = jnp.concatenate(sums, axis=0)
    high = value.astype(jnp.bfloat16)
    rest = value - high.astype(jnp.float32)
    mid = rest.astype(jnp.bfloat16)
    low = (rest - mid.astype(jnp.float32)).astype(jnp.bfloat16)
    out = jnp.zeros((24, 128), jnp.float32)
    for part in (low, mid, high):
        out = out + jnp.dot(part, weights, preferred_element_type=jnp.float32)
    return out


def fine_kernel(fs, fk, fr, strips, out, avg, stage_u, stage_k, stage_r, result, U, HZ, HX, HY, HT, KY, KX, RT, GH, sem_in, sem_out):
    loads = [load_patch(fs, fk, fr, p, stage_u, stage_k, stage_r, sem_in) for p in range(SLOT_DEV)]
    for group in loads:
        for copy in group:
            copy.start()
    stores = []
    for p in range(SLOT_DEV):
        for copy in loads[p]:
            copy.wait()
        patch_setup(p, stage_u, stage_k, stage_r, U, HZ, HX, HY, None, HT, KY, KX, RT)
        ghost_setup(strips[0, p], strips[1, p], GH)

        def step(k, carry):
            substep(k % 2, U, HZ, HX, HY, HT, KY, KX, RT, GH)
            return carry

        lax.fori_loop(0, RATIO, step, 0)
        for t in range(TILES):
            for s in range(3):
                for j in range(RATIO):
                    result[p, s, t, pl.ds(j, 8, stride=4), :] = U[0, s, j + 1, :, pl.ds(t * 128, 128)]
        for t in range(TILES):
            copy = pltpu.make_async_copy(result.at[p, :, t], out.at[p, :, :, pl.ds(t * 128, 128)], sem_out.at[p])
            copy.start()
            stores.append(copy)
        avg[p] = patch_average(0, U)
    for copy in stores:
        copy.wait()


def fine(fs, fk, fr, strips):
    f32 = jnp.float32
    hbm = pl.BlockSpec(memory_space=pl.ANY)
    vmem = pl.BlockSpec(memory_space=pltpu.VMEM)
    return pl.pallas_call(
        fine_kernel,
        out_shape=(
            jax.ShapeDtypeStruct((SLOT_DEV, 3, FZ, FXY), f32),
            jax.ShapeDtypeStruct((SLOT_DEV, 24, 128), f32),
        ),
        in_specs=[hbm, hbm, hbm, vmem],
        out_specs=(hbm, vmem),
        scratch_shapes=[
            pltpu.VMEM((SLOT_DEV, 3, TILES, FZ, 128), f32),
            pltpu.VMEM((SLOT_DEV, TILES, FZ, 128), f32),
            pltpu.VMEM((SLOT_DEV, TILES, FZ, 128), f32),
            pltpu.VMEM((SLOT_DEV, 3, TILES, FZ, 128), f32),
            pltpu.VMEM((2, 3, RATIO + 2, 8, FXY), f32),
            pltpu.VMEM((RATIO + 1, 8, FXY), f32),
            pltpu.VMEM((RATIO, 2, 8, FXY), f32),
            pltpu.VMEM((RATIO, 2, 8, FXY), f32),
            pltpu.VMEM((RATIO, 8, FXY), f32),
            pltpu.VMEM((RATIO, 8, FXY), f32),
            pltpu.VMEM((RATIO, 2, 8, 128), f32),
            pltpu.VMEM((RATIO, 8, FXY), f32),
            pltpu.VMEM((2, 3, TILES + 1, 8, 128), f32),
            pltpu.SemaphoreType.DMA((SLOT_DEV,)),
            pltpu.SemaphoreType.DMA((SLOT_DEV,)),
        ],
        compiler_params=pltpu.CompilerParams(vmem_limit_bytes=40 * 1024 * 1024),
    )(fs, fk, fr, strips)


def rim_rows(outer, block_cols, block_rows):
    species, planes, reach_x, cells_y = outer.shape
    padded_y = jnp.pad(outer, ((0, 0), (0, 0), (0, 0), (1, 1)))
    collected = []
    for column in range(block_cols):
        base_x = BLK * column
        lower_x = (
            outer[:, :, base_x, :].reshape(species, planes, block_rows, BLK).transpose(2, 0, 1, 3)
        )
        upper_x = (
            outer[:, :, base_x + BLK + 1, :]
            .reshape(species, planes, block_rows, BLK)
            .transpose(2, 0, 1, 3)
        )
        lower_y = padded_y[:, :, base_x + 1 : base_x + 1 + BLK, 0:cells_y:BLK].transpose(3, 0, 1, 2)
        upper_y = padded_y[
            :, :, base_x + 1 : base_x + 1 + BLK, BLK + 1 : cells_y + 2 : BLK
        ].transpose(3, 0, 1, 2)
        face_rows = jnp.stack([lower_x, upper_x, lower_y, upper_y], axis=1)
        collected.append(face_rows.reshape(block_rows, -1))
    return jnp.concatenate(collected, axis=0)


def sum_sources(received):
    return jnp.sum(received, axis=0)


def per_device(
    coarse_state, coarse_kappa, coarse_rate, fine_state, fine_kappa, fine_rate, boxes, cover
):
    af_count = lax.axis_size("af")
    af_index = lax.axis_index("af")
    col_index = lax.axis_index("col")
    slot_count = fine_state.shape[0]
    cells_x = coarse_state.shape[2]
    cells_y = coarse_state.shape[3]
    block_cols = cells_x // BLK
    block_rows = cells_y // BLK
    group_size = af_count * slot_count
    group_base = col_index * group_size
    stacked = jnp.concatenate([coarse_state, coarse_kappa[None]], axis=0)
    widened = with_halo(stacked, (("col", 3), ("af", 2)), 1)
    coarse_new = coarse_advance(widened[:3], widened[3], coarse_rate)
    outer_new = with_halo(coarse_new, (("af", 2),), 1)
    outer_old = widened[:3, :, :, 1:-1]
    group_boxes = lax.dynamic_slice_in_dim(boxes, group_base, group_size, 0)
    local_x = group_boxes[:, 0] - af_index * block_cols
    local_y = group_boxes[:, 1] - col_index * block_rows
    inside = (local_x >= 0) & (local_x < block_cols) & (local_y >= 0) & (local_y < block_rows)
    block_ids = jnp.where(inside, local_x * block_rows + local_y, -1)
    targets = (
        block_ids[:, None] == jnp.arange(block_cols * block_rows, dtype=jnp.int32)[None, :]
    ).astype(jnp.float32)
    earlier = rim_rows(outer_old, block_cols, block_rows)
    updated = rim_rows(outer_new, block_cols, block_rows)
    both = jnp.concatenate([earlier, updated], axis=1)
    send_rows = jnp.dot(targets, both, precision=lax.Precision.HIGHEST)
    received = lax.all_to_all(
        send_rows.reshape(af_count, slot_count, both.shape[1]), "af", split_axis=0, concat_axis=0, tiled=True
    )
    strips = sum_sources(received).reshape(slot_count, 2, 4, 3, NZC, BLK)
    strips = strips.transpose(1, 0, 4, 3, 2, 5).reshape(2, slot_count, NZC, 96)
    strips = jnp.pad(strips, ((0, 0), (0, 0), (0, 0), (0, 32)))
    fields, averages = fine(fine_state, fine_kappa, fine_rate, strips)
    averages = averages[:, :, :64].reshape(slot_count, -1)
    cover_mine = lax.dynamic_slice(
        cover, (af_index * block_cols, col_index * block_rows), (block_cols, block_rows)
    ).reshape(-1)
    wanted = cover_mine - group_base
    portion = lax.all_gather(averages, "af", axis=0, tiled=True)
    selector = (wanted[:, None] == jnp.arange(portion.shape[0], dtype=jnp.int32)[None, :]).astype(
        jnp.float32
    )
    placed = jnp.dot(selector, portion, precision=lax.Precision.HIGHEST)
    placed = (
        placed.reshape(block_cols, block_rows, 3, NZC, BLK, BLK)
        .transpose(2, 3, 0, 4, 1, 5)
        .reshape(3, NZC, cells_x, cells_y)
    )
    covered = (cover_mine >= 0).reshape(block_cols, block_rows)
    covered = jnp.repeat(jnp.repeat(covered, BLK, axis=0), BLK, axis=1)
    coarse_out = jnp.where(covered[None, None], placed, coarse_new)
    return (coarse_out, fields)


def solution(mesh):
    return jax.shard_map(
        per_device,
        mesh=mesh,
        in_specs=(
            P(None, None, "af", "col"),
            P(None, "af", "col"),
            P(None, "af", "col"),
            P(("col", "af"), None, None, None),
            P(("col", "af"), None, None),
            P(("col", "af"), None, None),
            P(),
            P(),
        ),
        out_specs=(P(None, None, "af", "col"), P(("col", "af"), None, None, None)),
        check_vma=False,
    )
```

```python
import jax
import jax.numpy as jnp
from jax import lax
from jax.experimental import pallas as pl
from jax.experimental.pallas import tpu as pltpu
from jax.sharding import PartitionSpec as P

NZC = 8
RATIO = 4
BLK = 8
SLOT_DEV = 4
N_AF = 32
N_COL = 4
FZ = 32
FXY = 1024
TILES = FXY // 128
FINE_DT = 1.0 / 112.0
FINE_SCALE = 16.0 / 112.0


DT_COARSE = 1.0 / 28.0
DIFFUSE = (1.0, 0.7, 0.45)


def lanes(shape=(8, 128)):
    return lax.broadcasted_iota(jnp.int32, shape, 1)


def rot(x, shift):
    return pltpu.roll(x, shift % x.shape[1], 1)


def face(p, q):
    both = p + q
    return (2.0 * FINE_SCALE) * p * q / both


def load_patch(fs, fk, fr, p, stage_u, stage_k, stage_r, sem):
    copies = []
    for t in range(TILES):
        cut = pl.ds(t * 128, 128)
        copies.append(pltpu.make_async_copy(fs.at[p, :, :, cut], stage_u.at[p, :, t], sem.at[p]))
        copies.append(pltpu.make_async_copy(fk.at[p, :, cut], stage_k.at[p, t], sem.at[p]))
        copies.append(pltpu.make_async_copy(fr.at[p, :, cut], stage_r.at[p, t], sem.at[p]))
    return copies


def patch_setup(p, stage_u, stage_k, stage_r, A, HZ, HX, HY, HT, KY, KX, RT):
    lane = lanes()
    col = lane % 32
    sub = lax.broadcasted_iota(jnp.int32, (8, 128), 0)
    zero = jnp.zeros((8, 128), jnp.float32)
    for t in range(TILES):
        cut = pl.ds(t * 128, 128)
        for s in range(3):
            for j in range(RATIO):
                A[s, j + 1, :, cut] = stage_u[p, s, t, pl.ds(j, 8, stride=4), :]
    for j in range(RATIO):
        cond = [stage_k[p, t, pl.ds(j, 8, stride=4), :] for t in range(TILES)]
        for t in range(TILES):
            cut = pl.ds(t * 128, 128)
            k = cond[t]
            RT[j, :, cut] = stage_r[p, t, pl.ds(j, 8, stride=4), :] * FINE_DT
            if j < RATIO - 1:
                HZ[j + 1, :, cut] = face(k, stage_k[p, t, pl.ds(j + 1, 8, stride=4), :])
            else:
                above = stage_k[p, t, pl.ds(0, 8, stride=4), :]
                up = jnp.where(sub == 7, 0.0, face(k, pltpu.roll(above, 7, 0)))
                HZ[RATIO, :, cut] = up
                HZ[0, :, cut] = jnp.where(sub == 0, 0.0, pltpu.roll(up, 1, 0))
            here = rot(k, -32)
            if t < TILES - 1:
                ahead = jnp.where(lane < 96, here, rot(cond[t + 1], -32))
                hx = face(k, ahead)
            else:
                hx = jnp.where(lane < 96, face(k, here), 0.0)
            HX[j, 0, :, cut] = hx
            hy = jnp.where(col == 31, 0.0, face(k, rot(k, -1)))
            HY[j, 0, :, cut] = hy
            HY[j, 1, :, cut] = jnp.where(col == 0, 0.0, rot(hy, 1))
            KY[j, :, cut] = jnp.where((col == 0) | (col == 31), k * FINE_SCALE, 0.0)
        KX[j, 0] = jnp.where(lane < 32, cond[0] * FINE_SCALE, 0.0)
        KX[j, 1] = jnp.where(lane >= 96, cond[TILES - 1] * FINE_SCALE, 0.0)
    for j in range(RATIO):
        last = zero
        for t in range(TILES):
            cut = pl.ds(t * 128, 128)
            moved = rot(HX[j, 0, :, cut], 32)
            behind = jnp.where(lane >= 32, moved, last)
            last = moved
            HX[j, 1, :, cut] = behind
            total = (HX[j, 0, :, cut] + behind) + (HY[j, 0, :, cut] + HY[j, 1, :, cut])
            total = total + (HZ[j, :, cut] + HZ[j + 1, :, cut]) + KY[j, :, cut]
            if t == 0:
                total = total + KX[j, 0]
            if t == TILES - 1:
                total = total + KX[j, 1]
            HT[j, :, cut] = total


def ghost_setup(old, new, GH):
    lane = lanes()
    delta = (new - old) * (1.0 / RATIO)
    for s in range(3):
        for t in range(TILES):
            pick = s * 32 + 16 + t + jnp.where(lane % 32 == 31, 8, 0)
            GH[0, s, t] = jnp.take_along_axis(old, pick, axis=1)
            GH[1, s, t] = jnp.take_along_axis(delta, pick, axis=1)
        pick = s * 32 + jnp.where(lane < 64, lane // 4, (lane - 96) // 4 + 8) % 16
        GH[0, s, TILES] = jnp.take_along_axis(old, pick, axis=1)
        GH[1, s, TILES] = jnp.take_along_axis(delta, pick, axis=1)


def substep(A, B, HZ, HX, HY, HT, KY, KX, RT, GH):
    lane = lanes()
    for s in range(3):
        A[s, 0] = pltpu.roll(A[s, RATIO], 1, 0)
        A[s, RATIO + 1] = pltpu.roll(A[s, 1], 7, 0)

    def plane(j, carry):
        for t in range(TILES):
            cut = pl.ds(t * 128, 128)
            hzu, hzd = HZ[j + 1, :, cut], HZ[j, :, cut]
            hxu, hxd = HX[j, 0, :, cut], HX[j, 1, :, cut]
            hyu, hyd = HY[j, 0, :, cut], HY[j, 1, :, cut]
            ht, ky, rt = HT[j, :, cut], KY[j, :, cut], RT[j, :, cut]
            us = [A[s, j + 1, :, cut] for s in range(3)]
            react = rt * (us[0] * us[1] - us[2])
            for s in range(3):
                u = us[s]
                up = rot(u, -32)
                if t < TILES - 1:
                    up = jnp.where(lane < 96, up, rot(A[s, j + 1, :, pl.ds(t * 128 + 128, 128)], -32))
                down = rot(u, 32)
                if t > 0:
                    down = jnp.where(lane >= 32, down, rot(A[s, j + 1, :, pl.ds(t * 128 - 128, 128)], 32))
                flow = (hzu * A[s, j + 2, :, cut] + hzd * A[s, j, :, cut]) + (hxu * up + hxd * down)
                flow = flow + (hyu * rot(u, -1) + hyd * rot(u, 1)) + (ky * GH[0, s, t] - ht * u)
                if t == 0:
                    flow = flow + KX[j, 0] * GH[0, s, TILES]
                if t == TILES - 1:
                    flow = flow + KX[j, 1] * GH[0, s, TILES]
                if s > 0:
                    flow = DIFFUSE[s] * flow
                B[s, j + 1, :, cut] = u + (flow - react if s < 2 else flow + react)
        return carry

    lax.fori_loop(0, RATIO, plane, 0)
    GH[0] = GH[0] + GH[1]


def patch_average(A):
    rows = lax.broadcasted_iota(jnp.int32, (FXY, 128), 0)
    cols = lax.broadcasted_iota(jnp.int32, (FXY, 128), 1)
    weights = jnp.where(cols == (rows // 128) * 8 + (rows % 32) // 4, 1.0 / 64.0, 0.0).astype(jnp.bfloat16)
    sums = [
        (A[s, 1] + A[s, 2]) + (A[s, 3] + A[s, 4]) for s in range(3)
    ]
    value = jnp.concatenate(sums, axis=0)
    high = value.astype(jnp.bfloat16)
    rest = value - high.astype(jnp.float32)
    mid = rest.astype(jnp.bfloat16)
    low = (rest - mid.astype(jnp.float32)).astype(jnp.bfloat16)
    out = jnp.zeros((24, 128), jnp.float32)
    for part in (low, mid, high):
        out = out + jnp.dot(part, weights, preferred_element_type=jnp.float32)
    return out


def fine_kernel(fs, fk, fr, strips, out, avg, stage_u, stage_k, stage_r, result, A, B, HZ, HX, HY, HT, KY, KX, RT, GH, sem_in, sem_out):
    loads = [load_patch(fs, fk, fr, p, stage_u, stage_k, stage_r, sem_in) for p in range(SLOT_DEV)]
    for group in loads:
        for copy in group:
            copy.start()
    stores = []
    for p in range(SLOT_DEV):
        for copy in loads[p]:
            copy.wait()
        patch_setup(p, stage_u, stage_k, stage_r, A, HZ, HX, HY, HT, KY, KX, RT)
        ghost_setup(strips[0, p], strips[1, p], GH)

        def step(k, carry):
            substep(A, B, HZ, HX, HY, HT, KY, KX, RT, GH)
            substep(B, A, HZ, HX, HY, HT, KY, KX, RT, GH)
            return carry

        lax.fori_loop(0, RATIO // 2, step, 0)
        for t in range(TILES):
            for s in range(3):
                for j in range(RATIO):
                    result[p, s, t, pl.ds(j, 8, stride=4), :] = A[s, j + 1, :, pl.ds(t * 128, 128)]
        for t in range(TILES):
            copy = pltpu.make_async_copy(result.at[p, :, t], out.at[p, :, :, pl.ds(t * 128, 128)], sem_out.at[p])
            copy.start()
            stores.append(copy)
        value = patch_average(A)
        if p % 2 == 0:
            even = value
        else:
            for s in range(3):
                cut = slice(s * 8, s * 8 + 8)
                avg[p // 2, s] = jnp.where(lanes() < 64, even[cut], rot(value[cut], 64))
    for copy in stores:
        copy.wait()


def fine(fs, fk, fr, strips):
    f32 = jnp.float32
    hbm = pl.BlockSpec(memory_space=pl.ANY)
    vmem = pl.BlockSpec(memory_space=pltpu.VMEM)
    return pl.pallas_call(
        fine_kernel,
        out_shape=(
            jax.ShapeDtypeStruct((SLOT_DEV, 3, FZ, FXY), f32),
            jax.ShapeDtypeStruct((SLOT_DEV // 2, 3, 8, 128), f32),
        ),
        in_specs=[hbm, hbm, hbm, vmem],
        out_specs=(hbm, vmem),
        scratch_shapes=[
            pltpu.VMEM((SLOT_DEV, 3, TILES, FZ, 128), f32),
            pltpu.VMEM((SLOT_DEV, TILES, FZ, 128), f32),
            pltpu.VMEM((SLOT_DEV, TILES, FZ, 128), f32),
            pltpu.VMEM((SLOT_DEV, 3, TILES, FZ, 128), f32),
            pltpu.VMEM((3, RATIO + 2, 8, FXY), f32),
            pltpu.VMEM((3, RATIO + 2, 8, FXY), f32),
            pltpu.VMEM((RATIO + 1, 8, FXY), f32),
            pltpu.VMEM((RATIO, 2, 8, FXY), f32),
            pltpu.VMEM((RATIO, 2, 8, FXY), f32),
            pltpu.VMEM((RATIO, 8, FXY), f32),
            pltpu.VMEM((RATIO, 8, FXY), f32),
            pltpu.VMEM((RATIO, 2, 8, 128), f32),
            pltpu.VMEM((RATIO, 8, FXY), f32),
            pltpu.VMEM((2, 3, TILES + 1, 8, 128), f32),
            pltpu.SemaphoreType.DMA((SLOT_DEV,)),
            pltpu.SemaphoreType.DMA((SLOT_DEV,)),
        ],
        compiler_params=pltpu.CompilerParams(vmem_limit_bytes=40 * 1024 * 1024),
    )(fs, fk, fr, strips)


MESH = pl.DeviceIdType.MESH


def signal_partners(barrier, with_col):
    af = lax.axis_index("af")

    def tell(o, carry):
        pl.semaphore_signal(barrier, inc=1, device_id={"af": lax.rem(af + o, N_AF)}, device_id_type=MESH)
        return carry

    lax.fori_loop(1, N_AF, tell, 0)
    if with_col:
        col = lax.axis_index("col")
        for step in (1, N_COL - 1):
            pl.semaphore_signal(
                barrier, inc=1, device_id={"col": lax.rem(col + step, N_COL)}, device_id_type=MESH
            )


def safe_face(p, q):
    both = p + q
    return (2.0 * DT_COARSE) * p * q / jnp.where(both > 0.0, both, 1.0)


def swap_groups(rows, steps):
    group = lanes() // 8
    rows = list(rows)
    for d in steps:
        keep = (group & d) == 0
        for i in range(len(rows)):
            if i & d == 0:
                a, b = rows[i], rows[i + d]
                rows[i] = jnp.where(keep, a, rot(b, 8 * d))
                rows[i + d] = jnp.where(keep, rot(a, -8 * d), b)
    return rows


def pack_strips(P, base, B):
    lane = lanes((8, 256))
    within = lane % 8
    for bx in range(2):
        for half in range(2):
            cut = pl.ds(half * 128, 128)
            rows = []
            for s in range(3):
                rows.append(P[s, base + BLK * bx - 1, :, cut])
                rows.append(P[s, base + BLK * bx + BLK, :, cut])
                for turn in (1, -BLK):
                    side = jnp.zeros((8, 128), jnp.float32)
                    for a in range(BLK):
                        moved = rot(P[s, base + BLK * bx + a], a + turn)[:, half * 128 : half * 128 + 128]
                        side = jnp.where(within[:, :128] == a, moved, side)
                    rows.append(side)
            rows += rows[:4]
            for g, row in enumerate(swap_groups(rows, (8, 4, 2, 1))):
                B[bx * 32 + half * 16 + g] = row


def pack_edges(C, E):
    lane = lanes()
    low = jnp.zeros((8, 128), jnp.float32)
    high = jnp.zeros((8, 128), jnp.float32)
    for q in range(4):
        for x in range(16):
            i = q * 16 + x
            low = jnp.where(lane == i, rot(C[q, x + 2, :, 0:128], i), low)
            high = jnp.where(lane == i, rot(C[q, x + 2, :, 128:256], i + 1), high)
    E[0] = low
    E[1] = high


def edge_change(own, beyond, inside):
    lane = lanes()
    coef = safe_face(own, beyond) * inside
    spread = jnp.where(
        lane < 16,
        rot(coef, -48),
        jnp.where(lane < 32, DIFFUSE[1] * rot(coef, -32), DIFFUSE[2] * rot(coef, -16)),
    )
    return spread * (beyond - own)


def coarse_update(C, N):
    lane = lanes((8, 256))
    sub = lax.broadcasted_iota(jnp.int32, (8, 256), 0)
    before = safe_face(C[3, 0], C[3, 1])
    for xi in range(1, 19):
        k = C[3, xi]
        rate = C[4, xi] * DT_COARSE
        after = safe_face(k, C[3, xi + 1])
        hzu = jnp.where(sub == 7, 0.0, safe_face(k, pltpu.roll(k, 7, 0)))
        hzd = jnp.where(sub == 0, 0.0, pltpu.roll(hzu, 1, 0))
        hyu = jnp.where(lane == 255, 0.0, safe_face(k, rot(k, -1)))
        hyd = jnp.where(lane == 0, 0.0, rot(hyu, 1))
        total = (hzu + hzd) + (before + after) + (hyu + hyd)
        us = [C[s, xi] for s in range(3)]
        react = rate * (us[0] * us[1] - us[2])
        for s in range(3):
            u = us[s]
            flow = (hzu * pltpu.roll(u, 7, 0) + hzd * pltpu.roll(u, 1, 0)) + (
                after * C[s, xi + 1] + before * C[s, xi - 1]
            )
            flow = flow + (hyu * rot(u, -1) + hyd * rot(u, 1)) - total * u
            if s > 0:
                flow = DIFFUSE[s] * flow
            N[s, xi - 1] = u + (flow - react if s < 2 else flow + react)
        before = after


def block_row(boxes, af, col, p):
    at = col * (N_AF * SLOT_DEV) + p
    x = boxes[0, at] - af * 2
    y = boxes[1, at] - col * 32
    return jnp.where((x >= 0) & (x < 2), jnp.clip(x * 32 + y, 0, 63), 64)


def send_strips(boxes, B, SEND, RECV, send_sem, recv_sem):
    af = lax.axis_index("af")
    col = lax.axis_index("col")
    for j in range(SLOT_DEV):
        RECV[0, j] = B[block_row(boxes, af, col, af * SLOT_DEV + j)]

    def one(o, carry):
        d = lax.rem(af + o, N_AF)
        for j in range(SLOT_DEV):
            SEND[o, j] = B[block_row(boxes, af, col, d * SLOT_DEV + j)]
        spread_copy(o, d, SEND, RECV, send_sem, recv_sem).start()
        return carry

    lax.fori_loop(1, N_AF, one, 0)


def spread_copy(o, d, SEND, RECV, send_sem, recv_sem):
    return pltpu.make_async_remote_copy(
        src_ref=SEND.at[o],
        dst_ref=RECV.at[o],
        send_sem=send_sem.at[o],
        recv_sem=recv_sem.at[o],
        device_id={"af": d},
        device_id_type=MESH,
    )


def wait_all(SEND, RECV, send_sem, recv_sem):
    af = lax.axis_index("af")

    def one(o, carry):
        copy = spread_copy(o, lax.rem(af + o, N_AF), SEND, RECV, send_sem, recv_sem)
        copy.wait_send()
        copy.wait_recv()
        return carry

    lax.fori_loop(1, N_AF, one, 0)


def coarse_kernel(cs, ck, cr, boxes, strips, cnew, C, N, E, B, SEND0, SEND1, RECV0, RECV1, halo_sem, s0, r0, s1, r1):
    af = lax.axis_index("af")
    col = lax.axis_index("col")
    barrier = pltpu.get_barrier_semaphore()
    signal_partners(barrier, True)
    for s in range(3):
        C[s, 2:18] = jnp.transpose(cs[s], (1, 0, 2))
    C[3, 2:18] = jnp.transpose(ck[...], (1, 0, 2))
    C[4, 2:18] = jnp.transpose(cr[...], (1, 0, 2))
    pl.semaphore_wait(barrier, N_AF + 1)

    def halo(src, dst, sem, where):
        return pltpu.make_async_remote_copy(
            src_ref=src, dst_ref=dst, send_sem=halo_sem.at[0, sem], recv_sem=halo_sem.at[1, sem],
            device_id=where, device_id_type=MESH,
        )

    right = halo(C.at[:, 16:18], C.at[:, 0:2], 0, {"af": lax.rem(af + 1, N_AF)})
    left = halo(C.at[:, 2:4], C.at[:, 18:20], 1, {"af": lax.rem(af + N_AF - 1, N_AF)})
    right.start()
    left.start()
    pack_edges(C, E)
    down = halo(E.at[0], E.at[3], 2, {"col": lax.rem(col + N_COL - 1, N_COL)})
    up = halo(E.at[1], E.at[2], 3, {"col": lax.rem(col + 1, N_COL)})
    down.start()
    up.start()
    B[64] = jnp.zeros((8, 128), jnp.float32)
    right.wait()
    left.wait()
    C[3, 0:2] = C[3, 0:2] * (af > 0).astype(jnp.float32)
    C[3, 18:20] = C[3, 18:20] * (af < N_AF - 1).astype(jnp.float32)
    pack_strips(C, 2, B)
    send_strips(boxes, B, SEND0, RECV0, s0, r0)
    coarse_update(C, N)
    pack_strips(N, 1, B)
    send_strips(boxes, B, SEND1, RECV1, s1, r1)
    down.wait()
    up.wait()
    lane = lanes()
    change_low = edge_change(E[0], E[2], (col > 0).astype(jnp.float32))
    change_high = edge_change(E[1], E[3], (col < N_COL - 1).astype(jnp.float32))
    for s in range(3):
        for x in range(16):
            i = s * 16 + x
            cnew[s, x, :, 0:128] = N[s, x + 1, :, 0:128] + jnp.where(lane == 0, rot(change_low, -i), 0.0)
            cnew[s, x, :, 128:256] = N[s, x + 1, :, 128:256] + jnp.where(lane == 127, rot(change_high, 127 - i), 0.0)
    wait_all(SEND0, RECV0, s0, r0)
    wait_all(SEND1, RECV1, s1, r1)
    for v, RECV in ((0, RECV0), (1, RECV1)):
        for j in range(SLOT_DEV):
            strips[v, j] = lax.fori_loop(1, N_AF, lambda o, total: total + RECV[o, j], RECV[0, j])


def coarse(cs, ck, cr, boxes):
    f32 = jnp.float32
    vmem = pl.BlockSpec(memory_space=pltpu.VMEM)
    return pl.pallas_call(
        coarse_kernel,
        out_shape=(
            jax.ShapeDtypeStruct((2, SLOT_DEV, 8, 128), f32),
            jax.ShapeDtypeStruct((3, 16, 8, 256), f32),
        ),
        in_specs=[vmem, vmem, vmem, pl.BlockSpec(memory_space=pltpu.SMEM)],
        out_specs=(vmem, vmem),
        scratch_shapes=[
            pltpu.VMEM((5, 20, 8, 256), f32),
            pltpu.VMEM((3, 18, 8, 256), f32),
            pltpu.VMEM((4, 8, 128), f32),
            pltpu.VMEM((65, 8, 128), f32),
        ]
        + [pltpu.VMEM((N_AF, SLOT_DEV, 8, 128), f32)] * 4
        + [pltpu.SemaphoreType.DMA((2, 4))]
        + [pltpu.SemaphoreType.DMA((N_AF,))] * 4,
        compiler_params=pltpu.CompilerParams(
            collective_id=0, has_side_effects=True, vmem_limit_bytes=32 * 1024 * 1024
        ),
    )(cs, ck, cr, boxes)


def place_averages(cover, RECV, cnew, T):
    af = lax.axis_index("af")
    col = lax.axis_index("col")
    lane = lanes()
    group = lane // 8
    for lx in range(2):
        for h in range(2):
            own = jnp.full((8, 128), -1, jnp.int32)
            where_at = []
            for g in range(16):
                p = cover[af * 2 + lx, col * 32 + h * 16 + g]
                own = jnp.where(group == g, p, own)
                q = jnp.maximum(p - col * (N_AF * SLOT_DEV), 0)
                source = lax.div(q, SLOT_DEV)
                slot = lax.rem(q, SLOT_DEV)
                at = lax.rem(af + N_AF - source, N_AF) * 2 + lax.div(slot, 2)
                where_at.append((at, lax.rem(slot, 2)))
            covered = own >= 0
            for s in range(3):
                rows = []
                for g in range(8):
                    at, odd = where_at[g]
                    first = RECV[at, s]
                    first = jnp.where(odd == 1, rot(first, 64), first)
                    at, odd = where_at[g + 8]
                    second = RECV[at, s]
                    second = jnp.where(odd == 1, second, rot(second, 64))
                    rows.append(jnp.where(lane < 64, first, second))
                for x, row in enumerate(swap_groups(rows, (4, 2, 1))):
                    cut = pl.ds(h * 128, 128)
                    T[s, lx * BLK + x, :, cut] = jnp.where(covered, row, cnew[s, lx * BLK + x, :, cut])


def average_kernel(avg, cnew, cover, out, T, RECV, send_sem, recv_sem):
    af = lax.axis_index("af")
    barrier = pltpu.get_barrier_semaphore()
    signal_partners(barrier, False)
    RECV[0:2] = avg[...]
    pl.semaphore_wait(barrier, N_AF - 1)

    def copy(o):
        return pltpu.make_async_remote_copy(
            src_ref=avg,
            dst_ref=RECV.at[pl.ds(o * 2, 2)],
            send_sem=send_sem.at[o],
            recv_sem=recv_sem.at[o],
            device_id={"af": lax.rem(af + o, N_AF)},
            device_id_type=MESH,
        )

    def begin(o, carry):
        copy(o).start()
        return carry

    def finish(o, carry):
        copy(o).wait_send()
        copy(o).wait_recv()
        return carry

    lax.fori_loop(1, N_AF, begin, 0)
    lax.fori_loop(1, N_AF, finish, 0)
    place_averages(cover, RECV, cnew, T)
    for s in range(3):
        out[s] = jnp.transpose(T[s], (1, 0, 2))


def averages_to_coarse(avg, cnew, cover):
    f32 = jnp.float32
    vmem = pl.BlockSpec(memory_space=pltpu.VMEM)
    return pl.pallas_call(
        average_kernel,
        out_shape=jax.ShapeDtypeStruct((3, NZC, 16, 256), f32),
        in_specs=[vmem, vmem, pl.BlockSpec(memory_space=pltpu.SMEM)],
        out_specs=vmem,
        scratch_shapes=[
            pltpu.VMEM((3, 16, 8, 256), f32),
            pltpu.VMEM((N_AF * 2, 3, 8, 128), f32),
            pltpu.SemaphoreType.DMA((N_AF,)),
            pltpu.SemaphoreType.DMA((N_AF,)),
        ],
        compiler_params=pltpu.CompilerParams(
            collective_id=1, has_side_effects=True, vmem_limit_bytes=32 * 1024 * 1024
        ),
    )(avg, cnew, cover)


def per_device(
    coarse_state, coarse_kappa, coarse_rate, fine_state, fine_kappa, fine_rate, boxes, cover
):
    strips, cnew = coarse(coarse_state, coarse_kappa, coarse_rate, boxes.T)
    fields, avg = fine(fine_state, fine_kappa, fine_rate, strips)
    return averages_to_coarse(avg, cnew, cover), fields


def solution(mesh):
    return jax.shard_map(
        per_device,
        mesh=mesh,
        in_specs=(
            P(None, None, "af", "col"),
            P(None, "af", "col"),
            P(None, "af", "col"),
            P(("col", "af"), None, None, None),
            P(("col", "af"), None, None),
            P(("col", "af"), None, None),
            P(),
            P(),
        ),
        out_specs=(P(None, None, "af", "col"), P(("col", "af"), None, None, None)),
        check_vma=False,
    )
```

```python
import jax
import jax.numpy as jnp
from jax import lax
from jax.experimental import pallas as pl
from jax.experimental.pallas import tpu as pltpu
from jax.sharding import PartitionSpec as P

NZC = 8
RATIO = 4
BLK = 8
SLOT_DEV = 4
N_AF = 32
N_COL = 4
FZ = 32
FXY = 1024
TILES = FXY // 128
FINE_DT = 1.0 / 112.0
FINE_SCALE = 16.0 / 112.0


DT_COARSE = 1.0 / 28.0
DIFFUSE = (1.0, 0.7, 0.45)


def lanes(shape=(8, 128)):
    return lax.broadcasted_iota(jnp.int32, shape, 1)


def rot(x, shift):
    return pltpu.roll(x, shift % x.shape[1], 1)


def face(p, q):
    both = p + q
    return (2.0 * FINE_SCALE) * p * q / both


def load_patch(fs, fk, fr, p, stage_u, stage_k, stage_r, sem):
    copies = []
    for t in range(TILES):
        cut = pl.ds(t * 128, 128)
        copies.append(pltpu.make_async_copy(fs.at[p, :, :, cut], stage_u.at[p, :, t], sem.at[p]))
        copies.append(pltpu.make_async_copy(fk.at[p, :, cut], stage_k.at[p, t], sem.at[p]))
        copies.append(pltpu.make_async_copy(fr.at[p, :, cut], stage_r.at[p, t], sem.at[p]))
    return copies


def store_patch(result, out, p, sem):
    return [
        pltpu.make_async_copy(result.at[p, :, t], out.at[p, :, :, pl.ds(t * 128, 128)], sem.at[p])
        for t in range(TILES)
    ]


def patch_setup(p, stage_u, stage_k, stage_r, A, HZ, HX, HY, HT, KY, KX, RT):
    lane = lanes()
    col = lane % 32
    sub = lax.broadcasted_iota(jnp.int32, (8, 128), 0)
    zero = jnp.zeros((8, 128), jnp.float32)
    for t in range(TILES):
        cut = pl.ds(t * 128, 128)
        for s in range(3):
            for j in range(RATIO):
                A[s, j + 1, :, cut] = stage_u[p, s, t, pl.ds(j, 8, stride=4), :]
    for j in range(RATIO):
        cond = [stage_k[p, t, pl.ds(j, 8, stride=4), :] for t in range(TILES)]
        for t in range(TILES):
            cut = pl.ds(t * 128, 128)
            k = cond[t]
            RT[j, :, cut] = stage_r[p, t, pl.ds(j, 8, stride=4), :] * FINE_DT
            if j < RATIO - 1:
                HZ[j + 1, :, cut] = face(k, stage_k[p, t, pl.ds(j + 1, 8, stride=4), :])
            else:
                above = stage_k[p, t, pl.ds(0, 8, stride=4), :]
                up = jnp.where(sub == 7, 0.0, face(k, pltpu.roll(above, 7, 0)))
                HZ[RATIO, :, cut] = up
                HZ[0, :, cut] = jnp.where(sub == 0, 0.0, pltpu.roll(up, 1, 0))
            here = rot(k, -32)
            if t < TILES - 1:
                ahead = jnp.where(lane < 96, here, rot(cond[t + 1], -32))
                hx = face(k, ahead)
            else:
                hx = jnp.where(lane < 96, face(k, here), 0.0)
            HX[j, 0, :, cut] = hx
            hy = jnp.where(col == 31, 0.0, face(k, rot(k, -1)))
            HY[j, 0, :, cut] = hy
            HY[j, 1, :, cut] = jnp.where(col == 0, 0.0, rot(hy, 1))
            KY[j, :, cut] = jnp.where((col == 0) | (col == 31), k * FINE_SCALE, 0.0)
        KX[j, 0] = jnp.where(lane < 32, cond[0] * FINE_SCALE, 0.0)
        KX[j, 1] = jnp.where(lane >= 96, cond[TILES - 1] * FINE_SCALE, 0.0)
    for j in range(RATIO):
        last = zero
        for t in range(TILES):
            cut = pl.ds(t * 128, 128)
            moved = rot(HX[j, 0, :, cut], 32)
            behind = jnp.where(lane >= 32, moved, last)
            last = moved
            HX[j, 1, :, cut] = behind
            total = (HX[j, 0, :, cut] + behind) + (HY[j, 0, :, cut] + HY[j, 1, :, cut])
            total = total + (HZ[j, :, cut] + HZ[j + 1, :, cut]) + KY[j, :, cut]
            if t == 0:
                total = total + KX[j, 0]
            if t == TILES - 1:
                total = total + KX[j, 1]
            HT[j, :, cut] = total


def ghost_tiles(strip, GH):
    lane = lanes()
    for s in range(3):
        for t in range(TILES):
            pick = s * 32 + 16 + t + jnp.where(lane % 32 == 31, 8, 0)
            GH[s, t] = jnp.take_along_axis(strip, pick, axis=1)
        pick = s * 32 + jnp.where(lane < 64, lane // 4, (lane - 96) // 4 + 8) % 16
        GH[s, TILES] = jnp.take_along_axis(strip, pick, axis=1)


def substep(A, B, HZ, HX, HY, HT, KY, KX, RT, GH):
    lane = lanes()
    for s in range(3):
        A[s, 0] = pltpu.roll(A[s, RATIO], 1, 0)
        A[s, RATIO + 1] = pltpu.roll(A[s, 1], 7, 0)

    def plane(j, carry):
        mid = [[A[s, j + 1, :, pl.ds(t * 128, 128)] for t in range(TILES)] for s in range(3)]
        ups = [[rot(u, -32) for u in mid[s]] for s in range(3)]
        downs = [[rot(u, 32) for u in mid[s]] for s in range(3)]
        for t in range(TILES):
            cut = pl.ds(t * 128, 128)
            hzu, hzd = HZ[j + 1, :, cut], HZ[j, :, cut]
            hxu, hxd = HX[j, 0, :, cut], HX[j, 1, :, cut]
            hyu, hyd = HY[j, 0, :, cut], HY[j, 1, :, cut]
            ht, ky, rt = HT[j, :, cut], KY[j, :, cut], RT[j, :, cut]
            us = [mid[s][t] for s in range(3)]
            react = rt * (us[0] * us[1] - us[2])
            for s in range(3):
                u = us[s]
                up = ups[s][t]
                if t < TILES - 1:
                    up = jnp.where(lane < 96, up, ups[s][t + 1])
                down = downs[s][t]
                if t > 0:
                    down = jnp.where(lane >= 32, down, downs[s][t - 1])
                flow = (hzu * A[s, j + 2, :, cut] + hzd * A[s, j, :, cut]) + (hxu * up + hxd * down)
                flow = flow + (hyu * rot(u, -1) + hyd * rot(u, 1)) + (ky * GH[s, t] - ht * u)
                if t == 0:
                    flow = flow + KX[j, 0] * GH[s, TILES]
                if t == TILES - 1:
                    flow = flow + KX[j, 1] * GH[s, TILES]
                if s > 0:
                    flow = DIFFUSE[s] * flow
                B[s, j + 1, :, cut] = u + (flow - react if s < 2 else flow + react)
        return carry

    for j in range(RATIO):
        plane(j, 0)


def patch_average(A):
    rows = lax.broadcasted_iota(jnp.int32, (FXY, 128), 0)
    cols = lax.broadcasted_iota(jnp.int32, (FXY, 128), 1)
    weights = jnp.where(cols == (rows // 128) * 8 + (rows % 32) // 4, 1.0 / 64.0, 0.0).astype(jnp.bfloat16)
    sums = [
        (A[s, 1] + A[s, 2]) + (A[s, 3] + A[s, 4]) for s in range(3)
    ]
    value = jnp.concatenate(sums, axis=0)
    high = value.astype(jnp.bfloat16)
    rest = value - high.astype(jnp.float32)
    mid = rest.astype(jnp.bfloat16)
    low = (rest - mid.astype(jnp.float32)).astype(jnp.bfloat16)
    out = jnp.zeros((24, 128), jnp.float32)
    for part in (low, mid, high):
        out = out + jnp.dot(part, weights, preferred_element_type=jnp.float32)
    return out


MESH = pl.DeviceIdType.MESH


def signal_partners(barrier, with_col):
    af = lax.axis_index("af")

    def tell(o, carry):
        pl.semaphore_signal(barrier, inc=1, device_id={"af": lax.rem(af + o, N_AF)}, device_id_type=MESH)
        return carry

    lax.fori_loop(1, N_AF, tell, 0)
    if with_col:
        col = lax.axis_index("col")
        for step in (1, N_COL - 1):
            pl.semaphore_signal(
                barrier, inc=1, device_id={"col": lax.rem(col + step, N_COL)}, device_id_type=MESH
            )


def safe_face(p, q):
    both = p + q
    return (2.0 * DT_COARSE) * p * q / jnp.where(both > 0.0, both, 1.0)


def swap_groups(rows, steps):
    group = lanes() // 8
    rows = list(rows)
    for d in steps:
        keep = (group & d) == 0
        for i in range(len(rows)):
            if i & d == 0:
                a, b = rows[i], rows[i + d]
                rows[i] = jnp.where(keep, a, rot(b, 8 * d))
                rows[i + d] = jnp.where(keep, rot(a, -8 * d), b)
    return rows


def pack_strips(P, base, B):
    lane = lanes((8, 256))
    within = lane % 8
    for bx in range(2):
        for half in range(2):
            cut = pl.ds(half * 128, 128)
            rows = []
            for s in range(3):
                rows.append(P[s, base + BLK * bx - 1, :, cut])
                rows.append(P[s, base + BLK * bx + BLK, :, cut])
                for turn in (1, -BLK):
                    side = jnp.zeros((8, 128), jnp.float32)
                    for a in range(BLK):
                        moved = rot(P[s, base + BLK * bx + a], a + turn)[:, half * 128 : half * 128 + 128]
                        side = jnp.where(within[:, :128] == a, moved, side)
                    rows.append(side)
            rows += rows[:4]
            for g, row in enumerate(swap_groups(rows, (8, 4, 2, 1))):
                B[bx * 32 + half * 16 + g] = row


def pack_edges(C, E):
    lane = lanes()
    low = jnp.zeros((8, 128), jnp.float32)
    high = jnp.zeros((8, 128), jnp.float32)
    for q in range(4):
        for x in range(16):
            i = q * 16 + x
            low = jnp.where(lane == i, rot(C[q, x + 2, :, 0:128], i), low)
            high = jnp.where(lane == i, rot(C[q, x + 2, :, 128:256], i + 1), high)
    E[0] = low
    E[1] = high


def edge_change(own, beyond, inside):
    lane = lanes()
    coef = safe_face(own, beyond) * inside
    spread = jnp.where(
        lane < 16,
        rot(coef, -48),
        jnp.where(lane < 32, DIFFUSE[1] * rot(coef, -32), DIFFUSE[2] * rot(coef, -16)),
    )
    return spread * (beyond - own)


def coarse_update(C, N):
    lane = lanes((8, 256))
    sub = lax.broadcasted_iota(jnp.int32, (8, 256), 0)
    before = safe_face(C[3, 0], C[3, 1])
    for xi in range(1, 19):
        k = C[3, xi]
        rate = C[4, xi] * DT_COARSE
        after = safe_face(k, C[3, xi + 1])
        hzu = jnp.where(sub == 7, 0.0, safe_face(k, pltpu.roll(k, 7, 0)))
        hzd = jnp.where(sub == 0, 0.0, pltpu.roll(hzu, 1, 0))
        hyu = jnp.where(lane == 255, 0.0, safe_face(k, rot(k, -1)))
        hyd = jnp.where(lane == 0, 0.0, rot(hyu, 1))
        total = (hzu + hzd) + (before + after) + (hyu + hyd)
        us = [C[s, xi] for s in range(3)]
        react = rate * (us[0] * us[1] - us[2])
        for s in range(3):
            u = us[s]
            flow = (hzu * pltpu.roll(u, 7, 0) + hzd * pltpu.roll(u, 1, 0)) + (
                after * C[s, xi + 1] + before * C[s, xi - 1]
            )
            flow = flow + (hyu * rot(u, -1) + hyd * rot(u, 1)) - total * u
            if s > 0:
                flow = DIFFUSE[s] * flow
            N[s, xi - 1] = u + (flow - react if s < 2 else flow + react)
        before = after


def block_row(boxes, af, col, p):
    at = col * (N_AF * SLOT_DEV) + p
    x = boxes[0, at] - af * 2
    y = boxes[1, at] - col * 32
    return jnp.where((x >= 0) & (x < 2), jnp.clip(x * 32 + y, 0, 63), 64)


def send_strips(boxes, B, SEND, RECV, send_sem, recv_sem):
    af = lax.axis_index("af")
    col = lax.axis_index("col")
    for j in range(SLOT_DEV):
        RECV[0, j] = B[block_row(boxes, af, col, af * SLOT_DEV + j)]

    def one(o, carry):
        d = lax.rem(af + o, N_AF)
        for j in range(SLOT_DEV):
            SEND[o, j] = B[block_row(boxes, af, col, d * SLOT_DEV + j)]
        spread_copy(o, d, SEND, RECV, send_sem, recv_sem).start()
        return carry

    lax.fori_loop(1, N_AF, one, 0)


def spread_copy(o, d, SEND, RECV, send_sem, recv_sem):
    return pltpu.make_async_remote_copy(
        src_ref=SEND.at[o],
        dst_ref=RECV.at[o],
        send_sem=send_sem.at[o],
        recv_sem=recv_sem.at[o],
        device_id={"af": d},
        device_id_type=MESH,
    )


def wait_all(SEND, RECV, send_sem, recv_sem):
    af = lax.axis_index("af")

    def one(o, carry):
        copy = spread_copy(o, lax.rem(af + o, N_AF), SEND, RECV, send_sem, recv_sem)
        copy.wait_send()
        copy.wait_recv()
        return carry

    lax.fori_loop(1, N_AF, one, 0)


def place_averages(cover, RECV, cnew, T):
    af = lax.axis_index("af")
    col = lax.axis_index("col")
    lane = lanes()
    group = lane // 8
    for lx in range(2):
        for h in range(2):
            own = jnp.full((8, 128), -1, jnp.int32)
            where_at = []
            for g in range(16):
                p = cover[af * 2 + lx, col * 32 + h * 16 + g]
                own = jnp.where(group == g, p, own)
                q = jnp.maximum(p - col * (N_AF * SLOT_DEV), 0)
                source = lax.div(q, SLOT_DEV)
                slot = lax.rem(q, SLOT_DEV)
                at = (lax.div(slot, 2), lax.rem(af + N_AF - source, N_AF))
                where_at.append((at, lax.rem(slot, 2)))
            covered = own >= 0
            for s in range(3):
                rows = []
                for g in range(8):
                    at, odd = where_at[g]
                    first = RECV[at[0], at[1], s]
                    first = jnp.where(odd == 1, rot(first, 64), first)
                    at, odd = where_at[g + 8]
                    second = RECV[at[0], at[1], s]
                    second = jnp.where(odd == 1, second, rot(second, 64))
                    rows.append(jnp.where(lane < 64, first, second))
                for x, row in enumerate(swap_groups(rows, (4, 2, 1))):
                    cut = pl.ds(h * 128, 128)
                    T[s, lx * BLK + x, :, cut] = jnp.where(covered, row, cnew[s, lx * BLK + x + 1, :, cut])


def total_of(RECV, j):
    return lax.fori_loop(1, N_AF, lambda o, total: total + RECV[o, j], RECV[0, j])


def kernel(
    cs, ck, cr, fs, fk, fr, boxes_in, cover_in, coarse_out, fine_out,
    boxes, cover, CI, C, N, T, E, BLOCKS, SEND0, SEND1, RECV0, RECV1, PAIR, AVG, RECVA,
    stage_u, stage_k, stage_r, result, A, B, HZ, HX, HY, HT, KY, KX, RT, GH, ST,
    load_sem, halo_sem, s0, r0, s1, r1, sa, ra, sem_in, sem_out,
):
    af = lax.axis_index("af")
    col = lax.axis_index("col")
    barrier = pltpu.get_barrier_semaphore()
    first = [
        pltpu.make_async_copy(cs, CI.at[0:3], load_sem.at[0]),
        pltpu.make_async_copy(ck, CI.at[3], load_sem.at[1]),
        pltpu.make_async_copy(cr, CI.at[4], load_sem.at[2]),
        pltpu.make_async_copy(boxes_in, boxes, load_sem.at[3]),
        pltpu.make_async_copy(cover_in, cover, load_sem.at[4]),
    ]
    for copy in first:
        copy.start()
    signal_partners(barrier, True)

    def begin_load(p, carry):
        for copy in load_patch(fs, fk, fr, p, stage_u, stage_k, stage_r, sem_in):
            copy.start()
        return carry

    lax.fori_loop(0, SLOT_DEV, begin_load, 0)
    for copy in first:
        copy.wait()
    for q in range(5):
        C[q, 2:18] = jnp.transpose(CI[q], (1, 0, 2))
    pl.semaphore_wait(barrier, N_AF + 1)

    def halo(src, dst, sem, where):
        return pltpu.make_async_remote_copy(
            src_ref=src, dst_ref=dst, send_sem=halo_sem.at[0, sem], recv_sem=halo_sem.at[1, sem],
            device_id=where, device_id_type=MESH,
        )

    right = halo(C.at[:, 16:18], C.at[:, 0:2], 0, {"af": lax.rem(af + 1, N_AF)})
    left = halo(C.at[:, 2:4], C.at[:, 18:20], 1, {"af": lax.rem(af + N_AF - 1, N_AF)})
    right.start()
    left.start()
    pack_edges(C, E)
    down = halo(E.at[0], E.at[3], 2, {"col": lax.rem(col + N_COL - 1, N_COL)})
    up = halo(E.at[1], E.at[2], 3, {"col": lax.rem(col + 1, N_COL)})
    down.start()
    up.start()
    BLOCKS[64] = jnp.zeros((8, 128), jnp.float32)
    right.wait()
    left.wait()
    C[3, 0:2] = C[3, 0:2] * (af > 0).astype(jnp.float32)
    C[3, 18:20] = C[3, 18:20] * (af < N_AF - 1).astype(jnp.float32)
    pack_strips(C, 2, BLOCKS)
    send_strips(boxes, BLOCKS, SEND0, RECV0, s0, r0)
    coarse_update(C, N)
    pack_strips(N, 1, BLOCKS)
    send_strips(boxes, BLOCKS, SEND1, RECV1, s1, r1)

    def prepare(p, carry):
        for copy in load_patch(fs, fk, fr, p, stage_u, stage_k, stage_r, sem_in):
            copy.wait()
        patch_setup(p, stage_u, stage_k, stage_r, A.at[p], HZ.at[p], HX.at[p], HY.at[p], HT.at[p], KY.at[p], KX.at[p], RT.at[p])
        return carry

    lax.fori_loop(0, SLOT_DEV, prepare, 0)
    wait_all(SEND0, RECV0, s0, r0)

    def opening(p, carry):
        ST[0, p] = total_of(RECV0, p)
        ghost_tiles(ST[0, p], GH.at[p])
        substep(A.at[p], B.at[p], HZ.at[p], HX.at[p], HY.at[p], HT.at[p], KY.at[p], KX.at[p], RT.at[p], GH.at[p])
        return carry

    lax.fori_loop(0, SLOT_DEV, opening, 0)
    wait_all(SEND1, RECV1, s1, r1)

    def average_copy(pair, o):
        return pltpu.make_async_remote_copy(
            src_ref=PAIR.at[pair],
            dst_ref=RECVA.at[pair, o],
            send_sem=sa.at[pair, o],
            recv_sem=ra.at[pair, o],
            device_id={"af": lax.rem(af + o, N_AF)},
            device_id_type=MESH,
        )

    def one_patch(p, carry):
        old = ST[0, p]
        change = (total_of(RECV1, p) - old) * (1.0 / RATIO)
        ghost_tiles(old + change, GH.at[p])
        substep(B.at[p], A.at[p], HZ.at[p], HX.at[p], HY.at[p], HT.at[p], KY.at[p], KX.at[p], RT.at[p], GH.at[p])
        ghost_tiles(old + 2.0 * change, GH.at[p])
        substep(A.at[p], B.at[p], HZ.at[p], HX.at[p], HY.at[p], HT.at[p], KY.at[p], KX.at[p], RT.at[p], GH.at[p])
        ghost_tiles(old + 3.0 * change, GH.at[p])
        substep(B.at[p], A.at[p], HZ.at[p], HX.at[p], HY.at[p], HT.at[p], KY.at[p], KX.at[p], RT.at[p], GH.at[p])
        for t in range(TILES):
            for s in range(3):
                for j in range(RATIO):
                    result[p, s, t, pl.ds(j, 8, stride=4), :] = A[p, s, j + 1, :, pl.ds(t * 128, 128)]
        for copy in store_patch(result, fine_out, p, sem_out):
            copy.start()
        value = patch_average(A.at[p])
        for s in range(3):
            AVG[p, s] = value[s * 8 : s * 8 + 8]
        return carry

    def two_patches(pair, carry):
        lax.fori_loop(2 * pair, 2 * pair + 2, one_patch, 0)
        for s in range(3):
            both = jnp.where(lanes() < 64, AVG[2 * pair, s], rot(AVG[2 * pair + 1, s], 64))
            PAIR[pair, s] = both
            RECVA[pair, 0, s] = both

        def begin(o, inner):
            average_copy(pair, o).start()
            return inner

        lax.fori_loop(1, N_AF, begin, 0)
        return carry

    lax.fori_loop(0, 2, two_patches, 0)
    down.wait()
    up.wait()
    lane = lanes()
    change_low = edge_change(E[0], E[2], (col > 0).astype(jnp.float32))
    change_high = edge_change(E[1], E[3], (col < N_COL - 1).astype(jnp.float32))
    for s in range(3):
        for x in range(16):
            i = s * 16 + x
            N[s, x + 1, :, 0:128] += jnp.where(lane == 0, rot(change_low, -i), 0.0)
            N[s, x + 1, :, 128:256] += jnp.where(lane == 127, rot(change_high, 127 - i), 0.0)

    def finish(o, carry):
        for pair in range(2):
            average_copy(pair, o).wait_send()
            average_copy(pair, o).wait_recv()
        return carry

    lax.fori_loop(1, N_AF, finish, 0)
    place_averages(cover, RECVA, N, T)
    for s in range(3):
        coarse_out[s] = jnp.transpose(T[s], (1, 0, 2))

    def end_store(p, carry):
        for copy in store_patch(result, fine_out, p, sem_out):
            copy.wait()
        return carry

    lax.fori_loop(0, SLOT_DEV, end_store, 0)


def per_device(
    coarse_state, coarse_kappa, coarse_rate, fine_state, fine_kappa, fine_rate, boxes, cover
):
    f32 = jnp.float32
    hbm = pl.BlockSpec(memory_space=pl.ANY)
    vmem = pl.BlockSpec(memory_space=pltpu.VMEM)
    D = SLOT_DEV
    message = pltpu.VMEM((N_AF, D, 8, 128), f32)
    sems = pltpu.SemaphoreType.DMA
    return pl.pallas_call(
        kernel,
        out_shape=(
            jax.ShapeDtypeStruct((3, NZC, 16, 256), f32),
            jax.ShapeDtypeStruct((D, 3, FZ, FXY), f32),
        ),
        in_specs=[hbm] * 8,
        out_specs=(vmem, hbm),
        scratch_shapes=[
            pltpu.SMEM((2, 512), jnp.int32),
            pltpu.SMEM((64, 128), jnp.int32),
            pltpu.VMEM((5, 8, 16, 256), f32),
            pltpu.VMEM((5, 20, 8, 256), f32),
            pltpu.VMEM((3, 18, 8, 256), f32),
            pltpu.VMEM((3, 16, 8, 256), f32),
            pltpu.VMEM((4, 8, 128), f32),
            pltpu.VMEM((65, 8, 128), f32),
            message,
            message,
            message,
            message,
            pltpu.VMEM((2, 3, 8, 128), f32),
            pltpu.VMEM((D, 3, 8, 128), f32),
            pltpu.VMEM((2, N_AF, 3, 8, 128), f32),
            pltpu.VMEM((D, 3, TILES, FZ, 128), f32),
            pltpu.VMEM((D, TILES, FZ, 128), f32),
            pltpu.VMEM((D, TILES, FZ, 128), f32),
            pltpu.VMEM((D, 3, TILES, FZ, 128), f32),
            pltpu.VMEM((D, 3, RATIO + 2, 8, FXY), f32),
            pltpu.VMEM((D, 3, RATIO + 2, 8, FXY), f32),
            pltpu.VMEM((D, RATIO + 1, 8, FXY), f32),
            pltpu.VMEM((D, RATIO, 2, 8, FXY), f32),
            pltpu.VMEM((D, RATIO, 2, 8, FXY), f32),
            pltpu.VMEM((D, RATIO, 8, FXY), f32),
            pltpu.VMEM((D, RATIO, 8, FXY), f32),
            pltpu.VMEM((D, RATIO, 2, 8, 128), f32),
            pltpu.VMEM((D, RATIO, 8, FXY), f32),
            pltpu.VMEM((D, 3, TILES + 1, 8, 128), f32),
            pltpu.VMEM((2, D, 8, 128), f32),
            sems((5,)),
            sems((2, 4)),
            sems((N_AF,)),
            sems((N_AF,)),
            sems((N_AF,)),
            sems((N_AF,)),
            sems((2, N_AF)),
            sems((2, N_AF)),
            sems((D,)),
            sems((D,)),
        ],
        compiler_params=pltpu.CompilerParams(
            collective_id=0, has_side_effects=True, vmem_limit_bytes=60 * 1024 * 1024
        ),
    )(coarse_state, coarse_kappa, coarse_rate, fine_state, fine_kappa, fine_rate, boxes.T, cover)


def solution(mesh):
    return jax.shard_map(
        per_device,
        mesh=mesh,
        in_specs=(
            P(None, None, "af", "col"),
            P(None, "af", "col"),
            P(None, "af", "col"),
            P(("col", "af"), None, None, None),
            P(("col", "af"), None, None),
            P(("col", "af"), None, None),
            P(),
            P(),
        ),
        out_specs=(P(None, None, "af", "col"), P(("col", "af"), None, None, None)),
        check_vma=False,
    )
```

```python
import jax
import jax.numpy as jnp
from jax import lax
from jax.experimental import pallas as pl
from jax.experimental.pallas import tpu as pltpu
from jax.sharding import PartitionSpec as P

NZC = 8
RATIO = 4
BLK = 8
SLOT_DEV = 4
N_AF = 32
N_COL = 4
FZ = 32
FXY = 1024
TILES = FXY // 128
FINE_DT = 1.0 / 112.0
FINE_SCALE = 16.0 / 112.0


DT_COARSE = 1.0 / 28.0
DIFFUSE = (1.0, 0.7, 0.45)


def lanes(shape=(8, 128)):
    return lax.broadcasted_iota(jnp.int32, shape, 1)


def rot(x, shift):
    return pltpu.roll(x, shift % x.shape[1], 1)


def face(p, q):
    both = p + q
    return (2.0 * FINE_SCALE) * p * q / both


def load_patch(fs, fk, fr, p, stage_u, stage_k, stage_r, sem):
    copies = []
    for t in range(TILES):
        cut = pl.ds(t * 128, 128)
        copies.append(pltpu.make_async_copy(fs.at[p, :, :, cut], stage_u.at[p, :, t], sem.at[p]))
        copies.append(pltpu.make_async_copy(fk.at[p, :, cut], stage_k.at[p, t], sem.at[p]))
        copies.append(pltpu.make_async_copy(fr.at[p, :, cut], stage_r.at[p, t], sem.at[p]))
    return copies


def store_patch(result, out, p, sem):
    return [
        pltpu.make_async_copy(result.at[p, :, t], out.at[p, :, :, pl.ds(t * 128, 128)], sem.at[p])
        for t in range(TILES)
    ]


def patch_setup(p, stage_u, stage_k, stage_r, A, HZ, HX, HY, HT, KY, KX, RT):
    lane = lanes()
    col = lane % 32
    sub = lax.broadcasted_iota(jnp.int32, (8, 128), 0)
    zero = jnp.zeros((8, 128), jnp.float32)
    for t in range(TILES):
        cut = pl.ds(t * 128, 128)
        for s in range(3):
            for j in range(RATIO):
                A[s, j + 1, :, cut] = stage_u[p, s, t, pl.ds(j, 8, stride=4), :]
    for j in range(RATIO):
        cond = [stage_k[p, t, pl.ds(j, 8, stride=4), :] for t in range(TILES)]
        for t in range(TILES):
            cut = pl.ds(t * 128, 128)
            k = cond[t]
            RT[j, :, cut] = stage_r[p, t, pl.ds(j, 8, stride=4), :] * FINE_DT
            if j < RATIO - 1:
                HZ[j + 1, :, cut] = face(k, stage_k[p, t, pl.ds(j + 1, 8, stride=4), :])
            else:
                above = stage_k[p, t, pl.ds(0, 8, stride=4), :]
                up = jnp.where(sub == 7, 0.0, face(k, pltpu.roll(above, 7, 0)))
                HZ[RATIO, :, cut] = up
                HZ[0, :, cut] = jnp.where(sub == 0, 0.0, pltpu.roll(up, 1, 0))
            here = rot(k, -32)
            if t < TILES - 1:
                ahead = jnp.where(lane < 96, here, rot(cond[t + 1], -32))
                hx = face(k, ahead)
            else:
                hx = jnp.where(lane < 96, face(k, here), 0.0)
            HX[j, 0, :, cut] = hx
            hy = jnp.where(col == 31, 0.0, face(k, rot(k, -1)))
            HY[j, 0, :, cut] = hy
            HY[j, 1, :, cut] = jnp.where(col == 0, 0.0, rot(hy, 1))
            KY[j, :, cut] = jnp.where((col == 0) | (col == 31), k * FINE_SCALE, 0.0)
        KX[j, 0] = jnp.where(lane < 32, cond[0] * FINE_SCALE, 0.0)
        KX[j, 1] = jnp.where(lane >= 96, cond[TILES - 1] * FINE_SCALE, 0.0)
    for j in range(RATIO):
        last = zero
        for t in range(TILES):
            cut = pl.ds(t * 128, 128)
            moved = rot(HX[j, 0, :, cut], 32)
            behind = jnp.where(lane >= 32, moved, last)
            last = moved
            HX[j, 1, :, cut] = behind
            total = (HX[j, 0, :, cut] + behind) + (HY[j, 0, :, cut] + HY[j, 1, :, cut])
            total = total + (HZ[j, :, cut] + HZ[j + 1, :, cut]) + KY[j, :, cut]
            if t == 0:
                total = total + KX[j, 0]
            if t == TILES - 1:
                total = total + KX[j, 1]
            HT[j, :, cut] = total


def ghost_tiles(strip, GH):
    lane = lanes()
    for s in range(3):
        for t in range(TILES):
            pick = s * 32 + 16 + t + jnp.where(lane % 32 == 31, 8, 0)
            GH[s, t] = jnp.take_along_axis(strip, pick, axis=1)
        pick = s * 32 + jnp.where(lane < 64, lane // 4, (lane - 96) // 4 + 8) % 16
        GH[s, TILES] = jnp.take_along_axis(strip, pick, axis=1)


def substep(A, B, HZ, HX, HY, HT, KY, KX, RT, GH):
    lane = lanes()
    for s in range(3):
        A[s, 0] = pltpu.roll(A[s, RATIO], 1, 0)
        A[s, RATIO + 1] = pltpu.roll(A[s, 1], 7, 0)

    def plane(j, carry):
        mid = [[A[s, j + 1, :, pl.ds(t * 128, 128)] for t in range(TILES)] for s in range(3)]
        ups = [[rot(u, -32) for u in mid[s]] for s in range(3)]
        downs = [[rot(u, 32) for u in mid[s]] for s in range(3)]
        for t in range(TILES):
            cut = pl.ds(t * 128, 128)
            hzu, hzd = HZ[j + 1, :, cut], HZ[j, :, cut]
            hxu, hxd = HX[j, 0, :, cut], HX[j, 1, :, cut]
            hyu, hyd = HY[j, 0, :, cut], HY[j, 1, :, cut]
            ht, ky, rt = HT[j, :, cut], KY[j, :, cut], RT[j, :, cut]
            us = [mid[s][t] for s in range(3)]
            react = rt * (us[0] * us[1] - us[2])
            for s in range(3):
                u = us[s]
                up = ups[s][t]
                if t < TILES - 1:
                    up = jnp.where(lane < 96, up, ups[s][t + 1])
                down = downs[s][t]
                if t > 0:
                    down = jnp.where(lane >= 32, down, downs[s][t - 1])
                flow = (hzu * A[s, j + 2, :, cut] + hzd * A[s, j, :, cut]) + (hxu * up + hxd * down)
                flow = flow + (hyu * rot(u, -1) + hyd * rot(u, 1)) + (ky * GH[s, t] - ht * u)
                if t == 0:
                    flow = flow + KX[j, 0] * GH[s, TILES]
                if t == TILES - 1:
                    flow = flow + KX[j, 1] * GH[s, TILES]
                if s > 0:
                    flow = DIFFUSE[s] * flow
                B[s, j + 1, :, cut] = u + (flow - react if s < 2 else flow + react)
        return carry

    for j in range(RATIO):
        plane(j, 0)


def average_weights(W):
    rows = lax.broadcasted_iota(jnp.int32, (FXY, 128), 0)
    cols = lax.broadcasted_iota(jnp.int32, (FXY, 128), 1)
    W[...] = jnp.where(cols == (rows // 128) * 8 + (rows % 32) // 4, 1.0 / 64.0, 0.0).astype(jnp.bfloat16)


def patch_average(A, W):
    sums = [
        (A[s, 1] + A[s, 2]) + (A[s, 3] + A[s, 4]) for s in range(3)
    ]
    value = jnp.concatenate(sums, axis=0)
    high = value.astype(jnp.bfloat16)
    rest = value - high.astype(jnp.float32)
    mid = rest.astype(jnp.bfloat16)
    low = (rest - mid.astype(jnp.float32)).astype(jnp.bfloat16)
    out = jnp.dot(jnp.concatenate([low, mid, high], axis=0), W[...], preferred_element_type=jnp.float32)
    return out[0:24] + out[24:48] + out[48:72]


MESH = pl.DeviceIdType.MESH


def signal_partners(barrier, with_col):
    af = lax.axis_index("af")

    def tell(o, carry):
        pl.semaphore_signal(barrier, inc=1, device_id={"af": lax.rem(af + o, N_AF)}, device_id_type=MESH)
        return carry

    lax.fori_loop(1, N_AF, tell, 0)
    if with_col:
        col = lax.axis_index("col")
        for step in (1, N_COL - 1):
            pl.semaphore_signal(
                barrier, inc=1, device_id={"col": lax.rem(col + step, N_COL)}, device_id_type=MESH
            )


def safe_face(p, q):
    both = p + q
    return (2.0 * DT_COARSE) * p * q / jnp.where(both > 0.0, both, 1.0)


def swap_groups(rows, steps):
    group = lanes() // 8
    rows = list(rows)
    for d in steps:
        keep = (group & d) == 0
        for i in range(len(rows)):
            if i & d == 0:
                a, b = rows[i], rows[i + d]
                rows[i] = jnp.where(keep, a, rot(b, 8 * d))
                rows[i + d] = jnp.where(keep, rot(a, -8 * d), b)
    return rows


def pack_strips(P, B):
    within = lanes((8, 256)) % 8
    for bx in range(2):
        sides = []
        for s in range(3):
            sides.append(P[s, 15 if bx == 0 else 7])
            sides.append(P[s, 8 if bx == 0 else 0])
            for turn in (1, -BLK):
                side = rot(P[s, BLK * bx], turn)
                for a in range(1, BLK):
                    side = jnp.where(within == a, rot(P[s, BLK * bx + a], a + turn), side)
                sides.append(side)
        for half in range(2):
            rows = [side[:, half * 128 : half * 128 + 128] for side in sides]
            rows += rows[:4]
            for g, row in enumerate(swap_groups(rows, (8, 4, 2, 1))):
                B[bx * 32 + half * 16 + g] = row


def pack_edges(C, E):
    lane = lanes()
    low = jnp.zeros((8, 128), jnp.float32)
    high = jnp.zeros((8, 128), jnp.float32)
    for q in range(4):
        for x in range(16):
            i = q * 16 + x
            low = jnp.where(lane == i, rot(C[q, x + 1, :, 0:128], i), low)
            high = jnp.where(lane == i, rot(C[q, x + 1, :, 128:256], i + 1), high)
    E[0] = low
    E[1] = high


def edge_change(own, beyond, inside):
    lane = lanes()
    coef = safe_face(own, beyond) * inside
    spread = jnp.where(
        lane < 16,
        rot(coef, -48),
        jnp.where(lane < 32, DIFFUSE[1] * rot(coef, -32), DIFFUSE[2] * rot(coef, -16)),
    )
    return spread * (beyond - own)


def coarse_update(C, N):
    lane = lanes((8, 256))
    sub = lax.broadcasted_iota(jnp.int32, (8, 256), 0)
    before = safe_face(C[3, 0], C[3, 1])
    for x in range(16):
        k = C[3, x + 1]
        rate = C[4, x + 1] * DT_COARSE
        after = safe_face(k, C[3, x + 2])
        hzu = jnp.where(sub == 7, 0.0, safe_face(k, pltpu.roll(k, 7, 0)))
        hzd = jnp.where(sub == 0, 0.0, pltpu.roll(hzu, 1, 0))
        hyu = jnp.where(lane == 255, 0.0, safe_face(k, rot(k, -1)))
        hyd = jnp.where(lane == 0, 0.0, rot(hyu, 1))
        total = (hzu + hzd) + (before + after) + (hyu + hyd)
        us = [C[s, x + 1] for s in range(3)]
        react = rate * (us[0] * us[1] - us[2])
        for s in range(3):
            u = us[s]
            flow = (hzu * pltpu.roll(u, 7, 0) + hzd * pltpu.roll(u, 1, 0)) + (
                after * C[s, x + 2] + before * C[s, x]
            )
            flow = flow + (hyu * rot(u, -1) + hyd * rot(u, 1)) - total * u
            if s > 0:
                flow = DIFFUSE[s] * flow
            N[s, x] = u + (flow - react if s < 2 else flow + react)
        before = after


def strip_tables(boxes, ROW, WHICH, MASK):
    af = lax.axis_index("af")
    col = lax.axis_index("col")

    def one(p, carry):
        at = col * (N_AF * SLOT_DEV) + p
        x = boxes[0, at] - af * 2 + 1
        y = boxes[1, at] - col * 32
        near = (x >= 0) & (x < 4)
        column = jnp.where((x == 1) | (x == 3), 0, 32)
        ROW[p] = jnp.clip(column + y, 0, 63)
        WHICH[p] = jnp.where(near, x, 4)
        return carry

    lax.fori_loop(0, N_AF * SLOT_DEV, one, 0)
    lane = lanes()
    side = (lane // 8) % 4
    used = lane < 96
    MASK[0] = jnp.where(used & (side == 1), 1.0, 0.0)
    MASK[1] = jnp.where(used & (side != 0), 1.0, 0.0)
    MASK[2] = jnp.where(used & (side != 1), 1.0, 0.0)
    MASK[3] = jnp.where(used & (side == 0), 1.0, 0.0)
    MASK[4] = jnp.zeros((8, 128), jnp.float32)


def fill_message(d, B, ROW, WHICH, MASK, OUT):
    lane = lanes()
    rows = []
    for j in range(SLOT_DEV):
        p = d * SLOT_DEV + j
        rows.append(rot(B[ROW[p]] * MASK[WHICH[p]], 96 * j))
    OUT[0] = jnp.where(lane < 96, rows[0], rows[1])
    OUT[1] = jnp.where(lane < 64, rows[1], rows[2])
    OUT[2] = jnp.where(lane < 32, rows[2], rows[3])


def fill_messages(B, ROW, WHICH, MASK, SEND, RECV, then):
    af = lax.axis_index("af")
    fill_message(af, B, ROW, WHICH, MASK, RECV.at[0])

    def one(o, carry):
        fill_message(lax.rem(af + o, N_AF), B, ROW, WHICH, MASK, SEND.at[o])
        then(o)
        return carry

    lax.fori_loop(1, N_AF, one, 0)


def sum_messages(RECV, ST):
    lane = lanes()

    def one(o, totals):
        return tuple(totals[i] + RECV[o, i] for i in range(3))

    a, b, c = lax.fori_loop(1, N_AF, one, (RECV[0, 0], RECV[0, 1], RECV[0, 2]))
    ST[0] = a
    ST[1] = rot(jnp.where(lane >= 96, a, b), -96)
    ST[2] = rot(jnp.where(lane >= 64, b, c), -64)
    ST[3] = rot(c, -32)


def spread_copy(o, d, SEND, RECV, send_sem, recv_sem):
    return pltpu.make_async_remote_copy(
        src_ref=SEND.at[o],
        dst_ref=RECV.at[o],
        send_sem=send_sem.at[o],
        recv_sem=recv_sem.at[o],
        device_id={"af": d},
        device_id_type=MESH,
    )


def wait_messages(SEND, RECV, send_sem, recv_sem, received):
    af = lax.axis_index("af")

    def one(o, carry):
        copy = spread_copy(o, lax.rem(af + o, N_AF), SEND, RECV, send_sem, recv_sem)
        if received:
            copy.wait_recv()
        else:
            copy.wait_send()
        return carry

    lax.fori_loop(1, N_AF, one, 0)


def place_tables(cover, PAIR_AT, FROM_AT, ODD, COVERED):
    af = lax.axis_index("af")
    col = lax.axis_index("col")
    group = lanes() // 8
    for lx in range(2):
        for h in range(2):
            own = jnp.full((8, 128), -1, jnp.int32)
            for g in range(16):
                p = cover[af * 2 + lx, col * 32 + h * 16 + g]
                own = jnp.where(group == g, p, own)
                q = jnp.clip(p - col * (N_AF * SLOT_DEV), 0, N_AF * SLOT_DEV - 1)
                source = lax.div(q, SLOT_DEV)
                slot = lax.rem(q, SLOT_DEV)
                at = (lx * 2 + h) * 16 + g
                PAIR_AT[at] = lax.div(slot, 2)
                FROM_AT[at] = lax.rem(af + N_AF - source, N_AF)
                ODD[at] = lax.rem(slot, 2)
            COVERED[lx * 2 + h] = jnp.where(own >= 0, 1.0, 0.0)


def place_averages(PAIR_AT, FROM_AT, ODD, COVERED, RECV, N, T):
    lane = lanes()
    for lx in range(2):
        for h in range(2):
            covered = COVERED[lx * 2 + h] > 0.0
            cut = pl.ds(h * 128, 128)
            for s in range(3):
                rows = []
                for g in range(8):
                    at = (lx * 2 + h) * 16 + g
                    first = RECV[PAIR_AT[at], FROM_AT[at], s]
                    first = jnp.where(ODD[at] == 1, rot(first, 64), first)
                    at = at + 8
                    second = RECV[PAIR_AT[at], FROM_AT[at], s]
                    second = jnp.where(ODD[at] == 1, second, rot(second, 64))
                    rows.append(jnp.where(lane < 64, first, second))
                for x, row in enumerate(swap_groups(rows, (4, 2, 1))):
                    T[s, lx * BLK + x, :, cut] = jnp.where(covered, row, N[s, lx * BLK + x, :, cut])


def kernel(
    cs, ck, cr, fs, fk, fr, boxes_in, cover_in, coarse_out, fine_out,
    boxes, cover, ROW, WHICH, PAIR_AT, FROM_AT, ODD, MASK, COVERED, W,
    CI, C, N, T, E, BLOCKS, SEND0, SEND1, RECV0, RECV1, PAIR, AVG, RECVA,
    stage_u, stage_k, stage_r, result, A, B, HZ, HX, HY, HT, KY, KX, RT, GH, ST,
    load_sem, halo_sem, s0, r0, s1, r1, sa, ra, sem_in, sem_out,
):
    af = lax.axis_index("af")
    col = lax.axis_index("col")
    barrier = pltpu.get_barrier_semaphore()
    first = [
        pltpu.make_async_copy(cs, CI.at[0:3], load_sem.at[0]),
        pltpu.make_async_copy(ck, CI.at[3], load_sem.at[1]),
        pltpu.make_async_copy(cr, CI.at[4], load_sem.at[2]),
        pltpu.make_async_copy(boxes_in, boxes, load_sem.at[3]),
        pltpu.make_async_copy(cover_in, cover, load_sem.at[4]),
    ]
    for copy in first:
        copy.start()
    signal_partners(barrier, True)

    def begin_load(p, carry):
        for copy in load_patch(fs, fk, fr, p, stage_u, stage_k, stage_r, sem_in):
            copy.start()
        return carry

    lax.fori_loop(0, SLOT_DEV, begin_load, 0)
    for copy in first:
        copy.wait()
    for q in range(5):
        C[q, 1:17] = jnp.transpose(CI[q], (1, 0, 2))
    pack_edges(C, E)
    strip_tables(boxes, ROW, WHICH, MASK)
    pack_strips(C.at[:, 1:17], BLOCKS)
    fill_messages(BLOCKS, ROW, WHICH, MASK, SEND0, RECV0, lambda o: None)
    pl.semaphore_wait(barrier, N_AF + 1)

    def halo(src, dst, sem, where):
        return pltpu.make_async_remote_copy(
            src_ref=src, dst_ref=dst, send_sem=halo_sem.at[0, sem], recv_sem=halo_sem.at[1, sem],
            device_id=where, device_id_type=MESH,
        )

    right = halo(C.at[0:4, 16], C.at[0:4, 0], 0, {"af": lax.rem(af + 1, N_AF)})
    left = halo(C.at[0:4, 1], C.at[0:4, 17], 1, {"af": lax.rem(af + N_AF - 1, N_AF)})
    right.start()
    left.start()

    def begin_old(o, carry):
        spread_copy(o, lax.rem(af + o, N_AF), SEND0, RECV0, s0, r0).start()
        return carry

    lax.fori_loop(1, N_AF, begin_old, 0)
    down = halo(E.at[0], E.at[3], 2, {"col": lax.rem(col + N_COL - 1, N_COL)})
    up = halo(E.at[1], E.at[2], 3, {"col": lax.rem(col + 1, N_COL)})
    down.start()
    up.start()

    def prepare(p, carry):
        for copy in load_patch(fs, fk, fr, p, stage_u, stage_k, stage_r, sem_in):
            copy.wait()
        patch_setup(p, stage_u, stage_k, stage_r, A.at[p], HZ.at[p], HX.at[p], HY.at[p], HT.at[p], KY.at[p], KX.at[p], RT.at[p])
        return carry

    lax.fori_loop(0, 2, prepare, 0)
    right.wait()
    left.wait()
    C[3, 0] = C[3, 0] * (af > 0).astype(jnp.float32)
    C[3, 17] = C[3, 17] * (af < N_AF - 1).astype(jnp.float32)
    coarse_update(C, N)
    pack_strips(N, BLOCKS)
    fill_messages(
        BLOCKS, ROW, WHICH, MASK, SEND1, RECV1,
        lambda o: spread_copy(o, lax.rem(af + o, N_AF), SEND1, RECV1, s1, r1).start(),
    )
    lax.fori_loop(2, SLOT_DEV, prepare, 0)
    average_weights(W)
    wait_messages(SEND0, RECV0, s0, r0, True)
    sum_messages(RECV0, ST.at[0])

    def opening(p, carry):
        ghost_tiles(ST[0, p], GH.at[p])
        substep(A.at[p], B.at[p], HZ.at[p], HX.at[p], HY.at[p], HT.at[p], KY.at[p], KX.at[p], RT.at[p], GH.at[p])
        return carry

    lax.fori_loop(0, SLOT_DEV, opening, 0)
    wait_messages(SEND1, RECV1, s1, r1, True)
    sum_messages(RECV1, ST.at[1])

    def average_copy(pair, o):
        return pltpu.make_async_remote_copy(
            src_ref=PAIR.at[pair],
            dst_ref=RECVA.at[pair, o],
            send_sem=sa.at[pair, o],
            recv_sem=ra.at[pair, o],
            device_id={"af": lax.rem(af + o, N_AF)},
            device_id_type=MESH,
        )

    def one_patch(p, carry):
        old = ST[0, p]
        change = (ST[1, p] - old) * (1.0 / RATIO)
        ghost_tiles(old + change, GH.at[p])
        substep(B.at[p], A.at[p], HZ.at[p], HX.at[p], HY.at[p], HT.at[p], KY.at[p], KX.at[p], RT.at[p], GH.at[p])
        ghost_tiles(old + 2.0 * change, GH.at[p])
        substep(A.at[p], B.at[p], HZ.at[p], HX.at[p], HY.at[p], HT.at[p], KY.at[p], KX.at[p], RT.at[p], GH.at[p])
        ghost_tiles(old + 3.0 * change, GH.at[p])
        substep(B.at[p], A.at[p], HZ.at[p], HX.at[p], HY.at[p], HT.at[p], KY.at[p], KX.at[p], RT.at[p], GH.at[p])
        value = patch_average(A.at[p], W)
        for s in range(3):
            AVG[p, s] = value[s * 8 : s * 8 + 8]
        return carry

    def write_patch(p, carry):
        for t in range(TILES):
            for s in range(3):
                for j in range(RATIO):
                    result[p, s, t, pl.ds(j, 8, stride=4), :] = A[p, s, j + 1, :, pl.ds(t * 128, 128)]
        for copy in store_patch(result, fine_out, p, sem_out):
            copy.start()
        return carry

    def two_patches(pair, carry):
        lax.fori_loop(2 * pair, 2 * pair + 2, one_patch, 0)
        for s in range(3):
            both = jnp.where(lanes() < 64, AVG[2 * pair, s], rot(AVG[2 * pair + 1, s], 64))
            PAIR[pair, s] = both
            RECVA[pair, 0, s] = both

        def begin(o, inner):
            average_copy(pair, o).start()
            return inner

        lax.fori_loop(1, N_AF, begin, 0)
        return carry

    lax.fori_loop(0, 2, two_patches, 0)
    lax.fori_loop(0, SLOT_DEV, write_patch, 0)
    down.wait()
    up.wait()
    lane = lanes()
    change_low = edge_change(E[0], E[2], (col > 0).astype(jnp.float32))
    change_high = edge_change(E[1], E[3], (col < N_COL - 1).astype(jnp.float32))
    for s in range(3):
        for x in range(16):
            i = s * 16 + x
            N[s, x, :, 0:128] += jnp.where(lane == 0, rot(change_low, -i), 0.0)
            N[s, x, :, 128:256] += jnp.where(lane == 127, rot(change_high, 127 - i), 0.0)
    place_tables(cover, PAIR_AT, FROM_AT, ODD, COVERED)
    wait_messages(SEND0, RECV0, s0, r0, False)
    wait_messages(SEND1, RECV1, s1, r1, False)

    def finish(o, carry):
        for pair in range(2):
            average_copy(pair, o).wait_send()
            average_copy(pair, o).wait_recv()
        return carry

    lax.fori_loop(1, N_AF, finish, 0)
    place_averages(PAIR_AT, FROM_AT, ODD, COVERED, RECVA, N, T)
    for s in range(3):
        coarse_out[s] = jnp.transpose(T[s], (1, 0, 2))

    def end_store(p, carry):
        for copy in store_patch(result, fine_out, p, sem_out):
            copy.wait()
        return carry

    lax.fori_loop(0, SLOT_DEV, end_store, 0)


def per_device(
    coarse_state, coarse_kappa, coarse_rate, fine_state, fine_kappa, fine_rate, boxes, cover
):
    f32 = jnp.float32
    hbm = pl.BlockSpec(memory_space=pl.ANY)
    vmem = pl.BlockSpec(memory_space=pltpu.VMEM)
    D = SLOT_DEV
    message = pltpu.VMEM((N_AF, 3, 8, 128), f32)
    table = pltpu.SMEM((128,), jnp.int32)
    sems = pltpu.SemaphoreType.DMA
    return pl.pallas_call(
        kernel,
        out_shape=(
            pltpu.VMEM((3, NZC, 16, 256), f32),
            pltpu.VMEM((D, 3, FZ, FXY), f32),
        ),
        in_specs=[hbm] * 8,
        out_specs=(vmem, vmem),
        scratch_shapes=[
            pltpu.SMEM((2, 512), jnp.int32),
            pltpu.SMEM((64, 128), jnp.int32),
            table,
            table,
            table,
            table,
            table,
            pltpu.VMEM((5, 8, 128), f32),
            pltpu.VMEM((4, 8, 128), f32),
            pltpu.VMEM((FXY, 128), jnp.bfloat16),
            pltpu.VMEM((5, 8, 16, 256), f32),
            pltpu.VMEM((5, 18, 8, 256), f32),
            pltpu.VMEM((3, 16, 8, 256), f32),
            pltpu.VMEM((3, 16, 8, 256), f32),
            pltpu.VMEM((4, 8, 128), f32),
            pltpu.VMEM((64, 8, 128), f32),
            message,
            message,
            message,
            message,
            pltpu.VMEM((2, 3, 8, 128), f32),
            pltpu.VMEM((D, 3, 8, 128), f32),
            pltpu.VMEM((2, N_AF, 3, 8, 128), f32),
            pltpu.VMEM((D, 3, TILES, FZ, 128), f32),
            pltpu.VMEM((D, TILES, FZ, 128), f32),
            pltpu.VMEM((D, TILES, FZ, 128), f32),
            pltpu.VMEM((D, 3, TILES, FZ, 128), f32),
            pltpu.VMEM((D, 3, RATIO + 2, 8, FXY), f32),
            pltpu.VMEM((D, 3, RATIO + 2, 8, FXY), f32),
            pltpu.VMEM((D, RATIO + 1, 8, FXY), f32),
            pltpu.VMEM((D, RATIO, 2, 8, FXY), f32),
            pltpu.VMEM((D, RATIO, 2, 8, FXY), f32),
            pltpu.VMEM((D, RATIO, 8, FXY), f32),
            pltpu.VMEM((D, RATIO, 8, FXY), f32),
            pltpu.VMEM((D, RATIO, 2, 8, 128), f32),
            pltpu.VMEM((D, RATIO, 8, FXY), f32),
            pltpu.VMEM((D, 3, TILES + 1, 8, 128), f32),
            pltpu.VMEM((2, D, 8, 128), f32),
            sems((5,)),
            sems((2, 4)),
            sems((N_AF,)),
            sems((N_AF,)),
            sems((N_AF,)),
            sems((N_AF,)),
            sems((2, N_AF)),
            sems((2, N_AF)),
            sems((D,)),
            sems((D,)),
        ],
        compiler_params=pltpu.CompilerParams(
            collective_id=0, has_side_effects=True, vmem_limit_bytes=60 * 1024 * 1024
        ),
    )(
        *[
            pltpu.with_memory_space_constraint(x, pltpu.HBM)
            for x in (coarse_state, coarse_kappa, coarse_rate, fine_state, fine_kappa, fine_rate, boxes.T, cover)
        ]
    )


def solution(mesh):
    return jax.shard_map(
        per_device,
        mesh=mesh,
        in_specs=(
            P(None, None, "af", "col"),
            P(None, "af", "col"),
            P(None, "af", "col"),
            P(("col", "af"), None, None, None),
            P(("col", "af"), None, None),
            P(("col", "af"), None, None),
            P(),
            P(),
        ),
        out_specs=(P(None, None, "af", "col"), P(("col", "af"), None, None, None)),
        check_vma=False,
    )
```

```python
import jax
import jax.numpy as jnp
from jax import lax
from jax.experimental import pallas as pl
from jax.experimental.pallas import tpu as pltpu
from jax.sharding import PartitionSpec as P

NZC = 8
RATIO = 4
BLK = 8
SLOT_DEV = 4
N_AF = 32
N_COL = 4
FZ = 32
FXY = 1024
TILES = FXY // 128
FINE_DT = 1.0 / 112.0
FINE_SCALE = 16.0 / 112.0


DT_COARSE = 1.0 / 28.0
DIFFUSE = (1.0, 0.7, 0.45)


def lanes(shape=(8, 128)):
    return lax.broadcasted_iota(jnp.int32, shape, 1)


def rot(x, shift):
    return pltpu.roll(x, shift % x.shape[1], 1)


def face(p, q):
    both = p + q
    return (2.0 * FINE_SCALE) * p * q / both


def load_patch(fs, fk, fr, p, stage_u, stage_k, stage_r, sem):
    copies = []
    for t in range(TILES):
        cut = pl.ds(t * 128, 128)
        copies.append(pltpu.make_async_copy(fs.at[p, :, :, cut], stage_u.at[p, :, t], sem.at[p]))
        copies.append(pltpu.make_async_copy(fk.at[p, :, cut], stage_k.at[p, t], sem.at[p]))
        copies.append(pltpu.make_async_copy(fr.at[p, :, cut], stage_r.at[p, t], sem.at[p]))
    return copies


def store_patch(result, out, p, sem):
    return [
        pltpu.make_async_copy(result.at[p, :, t], out.at[p, :, :, pl.ds(t * 128, 128)], sem.at[p])
        for t in range(TILES)
    ]


def patch_setup(p, stage_u, stage_k, stage_r, A, HZ, HX, HY, HT, KY, KX, RT):
    lane = lanes()
    col = lane % 32
    sub = lax.broadcasted_iota(jnp.int32, (8, 128), 0)
    zero = jnp.zeros((8, 128), jnp.float32)
    for t in range(TILES):
        cut = pl.ds(t * 128, 128)
        for s in range(3):
            for j in range(RATIO):
                A[s, j + 1, :, cut] = stage_u[p, s, t, pl.ds(j, 8, stride=4), :]
    for j in range(RATIO):
        cond = [stage_k[p, t, pl.ds(j, 8, stride=4), :] for t in range(TILES)]
        for t in range(TILES):
            cut = pl.ds(t * 128, 128)
            k = cond[t]
            RT[j, :, cut] = stage_r[p, t, pl.ds(j, 8, stride=4), :] * FINE_DT
            if j < RATIO - 1:
                HZ[j + 1, :, cut] = face(k, stage_k[p, t, pl.ds(j + 1, 8, stride=4), :])
            else:
                above = stage_k[p, t, pl.ds(0, 8, stride=4), :]
                up = jnp.where(sub == 7, 0.0, face(k, pltpu.roll(above, 7, 0)))
                HZ[RATIO, :, cut] = up
                HZ[0, :, cut] = jnp.where(sub == 0, 0.0, pltpu.roll(up, 1, 0))
            here = rot(k, -32)
            if t < TILES - 1:
                ahead = jnp.where(lane < 96, here, rot(cond[t + 1], -32))
                hx = face(k, ahead)
            else:
                hx = jnp.where(lane < 96, face(k, here), 0.0)
            HX[j, 0, :, cut] = hx
            hy = jnp.where(col == 31, 0.0, face(k, rot(k, -1)))
            HY[j, 0, :, cut] = hy
            HY[j, 1, :, cut] = jnp.where(col == 0, 0.0, rot(hy, 1))
            KY[j, :, cut] = jnp.where((col == 0) | (col == 31), k * FINE_SCALE, 0.0)
        KX[j, 0] = jnp.where(lane < 32, cond[0] * FINE_SCALE, 0.0)
        KX[j, 1] = jnp.where(lane >= 96, cond[TILES - 1] * FINE_SCALE, 0.0)
    for j in range(RATIO):
        last = zero
        for t in range(TILES):
            cut = pl.ds(t * 128, 128)
            moved = rot(HX[j, 0, :, cut], 32)
            behind = jnp.where(lane >= 32, moved, last)
            last = moved
            HX[j, 1, :, cut] = behind
            total = (HX[j, 0, :, cut] + behind) + (HY[j, 0, :, cut] + HY[j, 1, :, cut])
            total = total + (HZ[j, :, cut] + HZ[j + 1, :, cut]) + KY[j, :, cut]
            if t == 0:
                total = total + KX[j, 0]
            if t == TILES - 1:
                total = total + KX[j, 1]
            HT[j, :, cut] = total


def ghost_tiles(strip, GH):
    lane = lanes()
    for s in range(3):
        for t in range(TILES):
            pick = s * 32 + 16 + t + jnp.where(lane % 32 == 31, 8, 0)
            GH[s, t] = jnp.take_along_axis(strip, pick, axis=1)
        pick = s * 32 + jnp.where(lane < 64, lane // 4, (lane - 96) // 4 + 8) % 16
        GH[s, TILES] = jnp.take_along_axis(strip, pick, axis=1)


def substep(A, B, HZ, HX, HY, HT, KY, KX, RT, GH):
    lane = lanes()
    for s in range(3):
        A[s, 0] = pltpu.roll(A[s, RATIO], 1, 0)
        A[s, RATIO + 1] = pltpu.roll(A[s, 1], 7, 0)

    def plane(j, carry):
        mid = [[A[s, j + 1, :, pl.ds(t * 128, 128)] for t in range(TILES)] for s in range(3)]
        ups = [[rot(u, -32) for u in mid[s]] for s in range(3)]
        downs = [[rot(u, 32) for u in mid[s]] for s in range(3)]
        for t in range(TILES):
            cut = pl.ds(t * 128, 128)
            hzu, hzd = HZ[j + 1, :, cut], HZ[j, :, cut]
            hxu, hxd = HX[j, 0, :, cut], HX[j, 1, :, cut]
            hyu, hyd = HY[j, 0, :, cut], HY[j, 1, :, cut]
            ht, ky, rt = HT[j, :, cut], KY[j, :, cut], RT[j, :, cut]
            us = [mid[s][t] for s in range(3)]
            react = rt * (us[0] * us[1] - us[2])
            for s in range(3):
                u = us[s]
                up = ups[s][t]
                if t < TILES - 1:
                    up = jnp.where(lane < 96, up, ups[s][t + 1])
                down = downs[s][t]
                if t > 0:
                    down = jnp.where(lane >= 32, down, downs[s][t - 1])
                flow = (hzu * A[s, j + 2, :, cut] + hzd * A[s, j, :, cut]) + (hxu * up + hxd * down)
                flow = flow + (hyu * rot(u, -1) + hyd * rot(u, 1)) + (ky * GH[s, t] - ht * u)
                if t == 0:
                    flow = flow + KX[j, 0] * GH[s, TILES]
                if t == TILES - 1:
                    flow = flow + KX[j, 1] * GH[s, TILES]
                if s > 0:
                    flow = DIFFUSE[s] * flow
                B[s, j + 1, :, cut] = u + (flow - react if s < 2 else flow + react)
        return carry

    for j in range(RATIO):
        plane(j, 0)


def average_weights(W):
    rows = lax.broadcasted_iota(jnp.int32, (FXY, 128), 0)
    cols = lax.broadcasted_iota(jnp.int32, (FXY, 128), 1)
    W[...] = jnp.where(cols == (rows // 128) * 8 + (rows % 32) // 4, 1.0 / 64.0, 0.0).astype(jnp.bfloat16)


def patch_average(A, W):
    sums = [
        (A[s, 1] + A[s, 2]) + (A[s, 3] + A[s, 4]) for s in range(3)
    ]
    value = jnp.concatenate(sums, axis=0)
    high = value.astype(jnp.bfloat16)
    rest = value - high.astype(jnp.float32)
    mid = rest.astype(jnp.bfloat16)
    low = (rest - mid.astype(jnp.float32)).astype(jnp.bfloat16)
    out = jnp.dot(jnp.concatenate([low, mid, high], axis=0), W[...], preferred_element_type=jnp.float32)
    return out[0:24] + out[24:48] + out[48:72]


MESH = pl.DeviceIdType.MESH


def signal_partners(barrier, with_col):
    af = lax.axis_index("af")

    def tell(o, carry):
        pl.semaphore_signal(barrier, inc=1, device_id={"af": lax.rem(af + o, N_AF)}, device_id_type=MESH)
        return carry

    lax.fori_loop(1, N_AF, tell, 0)
    if with_col:
        col = lax.axis_index("col")
        for step in (1, N_COL - 1):
            pl.semaphore_signal(
                barrier, inc=1, device_id={"col": lax.rem(col + step, N_COL)}, device_id_type=MESH
            )


def safe_face(p, q):
    both = p + q
    return (2.0 * DT_COARSE) * p * q / jnp.where(both > 0.0, both, 1.0)


def swap_groups(rows, steps):
    group = lanes() // 8
    rows = list(rows)
    for d in steps:
        keep = (group & d) == 0
        for i in range(len(rows)):
            if i & d == 0:
                a, b = rows[i], rows[i + d]
                rows[i] = jnp.where(keep, a, rot(b, 8 * d))
                rows[i + d] = jnp.where(keep, rot(a, -8 * d), b)
    return rows


def pack_strips(P, B):
    within = lanes((8, 256)) % 8
    for bx in range(2):
        sides = []
        for s in range(3):
            sides.append(P[s, 15 if bx == 0 else 7])
            sides.append(P[s, 8 if bx == 0 else 0])
            for turn in (1, -BLK):
                side = rot(P[s, BLK * bx], turn)
                for a in range(1, BLK):
                    side = jnp.where(within == a, rot(P[s, BLK * bx + a], a + turn), side)
                sides.append(side)
        for half in range(2):
            rows = [side[:, half * 128 : half * 128 + 128] for side in sides]
            rows += rows[:4]
            for g, row in enumerate(swap_groups(rows, (8, 4, 2, 1))):
                B[bx * 32 + half * 16 + g] = row


def pack_edges(C, E):
    lane = lanes()
    low = jnp.zeros((8, 128), jnp.float32)
    high = jnp.zeros((8, 128), jnp.float32)
    for q in range(4):
        for x in range(16):
            i = q * 16 + x
            low = jnp.where(lane == i, rot(C[q, x + 1, :, 0:128], i), low)
            high = jnp.where(lane == i, rot(C[q, x + 1, :, 128:256], i + 1), high)
    E[0] = low
    E[1] = high


def edge_change(own, beyond, inside):
    lane = lanes()
    coef = safe_face(own, beyond) * inside
    spread = jnp.where(
        lane < 16,
        rot(coef, -48),
        jnp.where(lane < 32, DIFFUSE[1] * rot(coef, -32), DIFFUSE[2] * rot(coef, -16)),
    )
    return spread * (beyond - own)


def coarse_update(C, N):
    lane = lanes((8, 256))
    sub = lax.broadcasted_iota(jnp.int32, (8, 256), 0)
    before = safe_face(C[3, 0], C[3, 1])
    for x in range(16):
        k = C[3, x + 1]
        rate = C[4, x + 1] * DT_COARSE
        after = safe_face(k, C[3, x + 2])
        hzu = jnp.where(sub == 7, 0.0, safe_face(k, pltpu.roll(k, 7, 0)))
        hzd = jnp.where(sub == 0, 0.0, pltpu.roll(hzu, 1, 0))
        hyu = jnp.where(lane == 255, 0.0, safe_face(k, rot(k, -1)))
        hyd = jnp.where(lane == 0, 0.0, rot(hyu, 1))
        total = (hzu + hzd) + (before + after) + (hyu + hyd)
        us = [C[s, x + 1] for s in range(3)]
        react = rate * (us[0] * us[1] - us[2])
        for s in range(3):
            u = us[s]
            flow = (hzu * pltpu.roll(u, 7, 0) + hzd * pltpu.roll(u, 1, 0)) + (
                after * C[s, x + 2] + before * C[s, x]
            )
            flow = flow + (hyu * rot(u, -1) + hyd * rot(u, 1)) - total * u
            if s > 0:
                flow = DIFFUSE[s] * flow
            N[s, x] = u + (flow - react if s < 2 else flow + react)
        before = after


def strip_tables(boxes, ROW, WHICH, MASK):
    af = lax.axis_index("af")
    col = lax.axis_index("col")

    def eight(i, carry):
        for q in range(8):
            p = i * 8 + q
            at = col * (N_AF * SLOT_DEV) + p
            x = boxes[0, at] - af * 2 + 1
            y = boxes[1, at] - col * 32
            near = (x >= 0) & (x < 4)
            column = jnp.where((x == 1) | (x == 3), 0, 32)
            ROW[p] = jnp.clip(column + y, 0, 63)
            WHICH[p] = jnp.where(near, x, 4)
        return carry

    lax.fori_loop(0, N_AF * SLOT_DEV // 8, eight, 0)
    lane = lanes()
    side = (lane // 8) % 4
    used = lane < 96
    MASK[0] = jnp.where(used & (side == 1), 1.0, 0.0)
    MASK[1] = jnp.where(used & (side != 0), 1.0, 0.0)
    MASK[2] = jnp.where(used & (side != 1), 1.0, 0.0)
    MASK[3] = jnp.where(used & (side == 0), 1.0, 0.0)
    MASK[4] = jnp.zeros((8, 128), jnp.float32)


def fill_message(d, B, ROW, WHICH, MASK, OUT):
    lane = lanes()
    rows = []
    for j in range(SLOT_DEV):
        p = d * SLOT_DEV + j
        rows.append(rot(B[ROW[p]] * MASK[WHICH[p]], 96 * j))
    OUT[0] = jnp.where(lane < 96, rows[0], rows[1])
    OUT[1] = jnp.where(lane < 64, rows[1], rows[2])
    OUT[2] = jnp.where(lane < 32, rows[2], rows[3])


def fill_messages(B, ROW, WHICH, MASK, SEND, RECV, send_sem, recv_sem):
    af = lax.axis_index("af")

    def four(i, carry):
        for q in range(4):
            o = i * 4 + q
            fill_message(lax.rem(af + o, N_AF), B, ROW, WHICH, MASK, SEND.at[o])
        for q in range(4):
            o = i * 4 + q

            @pl.when(o > 0)
            def start():
                spread_copy(o, lax.rem(af + o, N_AF), SEND, RECV, send_sem, recv_sem).start()

        return carry

    lax.fori_loop(0, N_AF // 4, four, 0)
    RECV[0] = SEND[0]


def sum_messages(RECV, ST):
    lane = lanes()

    def one(o, totals):
        return tuple(totals[i] + RECV[o, i] for i in range(3))

    a, b, c = lax.fori_loop(1, N_AF, one, (RECV[0, 0], RECV[0, 1], RECV[0, 2]))
    ST[0] = a
    ST[1] = rot(jnp.where(lane >= 96, a, b), -96)
    ST[2] = rot(jnp.where(lane >= 64, b, c), -64)
    ST[3] = rot(c, -32)


def spread_copy(o, d, SEND, RECV, send_sem, recv_sem):
    return pltpu.make_async_remote_copy(
        src_ref=SEND.at[o],
        dst_ref=RECV.at[o],
        send_sem=send_sem,
        recv_sem=recv_sem,
        device_id={"af": d},
        device_id_type=MESH,
    )


def wait_messages(RECV, send_sem, recv_sem, received):
    af = lax.axis_index("af")
    whole = RECV.at[pl.ds(1, N_AF - 1)]
    copy = pltpu.make_async_remote_copy(
        src_ref=whole,
        dst_ref=whole,
        send_sem=send_sem,
        recv_sem=recv_sem,
        device_id={"af": lax.rem(af + 1, N_AF)},
        device_id_type=MESH,
    )
    if received:
        copy.wait_recv()
    else:
        copy.wait_send()


def place_tables(cover, PAIR_AT, FROM_AT, ODD, COVERED):
    af = lax.axis_index("af")
    col = lax.axis_index("col")
    group = lanes() // 8
    for lx in range(2):
        for h in range(2):
            own = jnp.full((8, 128), -1, jnp.int32)
            for g in range(16):
                p = cover[af * 2 + lx, col * 32 + h * 16 + g]
                own = jnp.where(group == g, p, own)
                q = jnp.clip(p - col * (N_AF * SLOT_DEV), 0, N_AF * SLOT_DEV - 1)
                source = lax.div(q, SLOT_DEV)
                slot = lax.rem(q, SLOT_DEV)
                at = (lx * 2 + h) * 16 + g
                PAIR_AT[at] = lax.div(slot, 2)
                FROM_AT[at] = lax.rem(af + N_AF - source, N_AF)
                ODD[at] = lax.rem(slot, 2)
            COVERED[lx * 2 + h] = jnp.where(own >= 0, 1.0, 0.0)


def place_averages(PAIR_AT, FROM_AT, ODD, COVERED, RECV, N, T):
    lane = lanes()
    for lx in range(2):
        for h in range(2):
            covered = COVERED[lx * 2 + h] > 0.0
            cut = pl.ds(h * 128, 128)
            for s in range(3):
                rows = []
                for g in range(8):
                    at = (lx * 2 + h) * 16 + g
                    first = RECV[PAIR_AT[at], FROM_AT[at], s]
                    first = jnp.where(ODD[at] == 1, rot(first, 64), first)
                    at = at + 8
                    second = RECV[PAIR_AT[at], FROM_AT[at], s]
                    second = jnp.where(ODD[at] == 1, second, rot(second, 64))
                    rows.append(jnp.where(lane < 64, first, second))
                for x, row in enumerate(swap_groups(rows, (4, 2, 1))):
                    T[s, lx * BLK + x, :, cut] = jnp.where(covered, row, N[s, lx * BLK + x, :, cut])


def kernel(
    cs, ck, cr, fs, fk, fr, boxes_in, cover_in, coarse_out, fine_out,
    boxes, cover, ROW, WHICH, PAIR_AT, FROM_AT, ODD, MASK, COVERED, W,
    CI, C, N, T, E, BLOCKS, SEND0, SEND1, RECV0, RECV1, PAIR, AVG, RECVA,
    stage_u, stage_k, stage_r, result, A, B, HZ, HX, HY, HT, KY, KX, RT, GH, ST,
    load_sem, halo_sem, exchange, averaged, sem_in, sem_out,
):
    af = lax.axis_index("af")
    col = lax.axis_index("col")
    barrier = pltpu.get_barrier_semaphore()
    first = [
        pltpu.make_async_copy(cs, CI.at[0:3], load_sem.at[0]),
        pltpu.make_async_copy(ck, CI.at[3], load_sem.at[1]),
        pltpu.make_async_copy(cr, CI.at[4], load_sem.at[2]),
        pltpu.make_async_copy(boxes_in, boxes, load_sem.at[3]),
        pltpu.make_async_copy(cover_in, cover, load_sem.at[4]),
    ]
    for copy in first:
        copy.start()
    signal_partners(barrier, True)

    def begin_load(p, carry):
        for copy in load_patch(fs, fk, fr, p, stage_u, stage_k, stage_r, sem_in):
            copy.start()
        return carry

    lax.fori_loop(0, SLOT_DEV, begin_load, 0)
    for copy in first:
        copy.wait()
    for q in range(5):
        C[q, 1:17] = jnp.transpose(CI[q], (1, 0, 2))
    pl.semaphore_wait(barrier, N_AF + 1)

    def halo(src, dst, sem, where):
        return pltpu.make_async_remote_copy(
            src_ref=src, dst_ref=dst, send_sem=halo_sem.at[0, sem], recv_sem=halo_sem.at[1, sem],
            device_id=where, device_id_type=MESH,
        )

    right = halo(C.at[0:4, 16], C.at[0:4, 0], 0, {"af": lax.rem(af + 1, N_AF)})
    left = halo(C.at[0:4, 1], C.at[0:4, 17], 1, {"af": lax.rem(af + N_AF - 1, N_AF)})
    right.start()
    left.start()

    strip_tables(boxes, ROW, WHICH, MASK)
    pack_strips(C.at[:, 1:17], BLOCKS)
    fill_messages(BLOCKS, ROW, WHICH, MASK, SEND0, RECV0, exchange.at[0], exchange.at[1])

    def prepare(p, carry):
        for copy in load_patch(fs, fk, fr, p, stage_u, stage_k, stage_r, sem_in):
            copy.wait()
        patch_setup(p, stage_u, stage_k, stage_r, A.at[p], HZ.at[p], HX.at[p], HY.at[p], HT.at[p], KY.at[p], KX.at[p], RT.at[p])
        return carry

    right.wait()
    left.wait()
    C[3, 0] = C[3, 0] * (af > 0).astype(jnp.float32)
    C[3, 17] = C[3, 17] * (af < N_AF - 1).astype(jnp.float32)
    coarse_update(C, N)
    pack_strips(N, BLOCKS)
    fill_messages(BLOCKS, ROW, WHICH, MASK, SEND1, RECV1, exchange.at[2], exchange.at[3])
    pack_edges(C, E)
    down = halo(E.at[0], E.at[3], 2, {"col": lax.rem(col + N_COL - 1, N_COL)})
    up = halo(E.at[1], E.at[2], 3, {"col": lax.rem(col + 1, N_COL)})
    down.start()
    up.start()
    lax.fori_loop(0, SLOT_DEV, prepare, 0)
    average_weights(W)
    wait_messages(RECV0, exchange.at[0], exchange.at[1], True)
    sum_messages(RECV0, ST.at[0])

    def opening(p, carry):
        ghost_tiles(ST[0, p], GH.at[p])
        substep(A.at[p], B.at[p], HZ.at[p], HX.at[p], HY.at[p], HT.at[p], KY.at[p], KX.at[p], RT.at[p], GH.at[p])
        return carry

    lax.fori_loop(0, SLOT_DEV, opening, 0)
    wait_messages(RECV1, exchange.at[2], exchange.at[3], True)
    sum_messages(RECV1, ST.at[1])

    def average_copy(pair, o):
        return pltpu.make_async_remote_copy(
            src_ref=PAIR.at[pair],
            dst_ref=RECVA.at[pair, o],
            send_sem=averaged.at[0, pair],
            recv_sem=averaged.at[1, pair],
            device_id={"af": lax.rem(af + o, N_AF)},
            device_id_type=MESH,
        )

    def one_patch(p, carry):
        old = ST[0, p]
        change = (ST[1, p] - old) * (1.0 / RATIO)
        ghost_tiles(old + change, GH.at[p])
        substep(B.at[p], A.at[p], HZ.at[p], HX.at[p], HY.at[p], HT.at[p], KY.at[p], KX.at[p], RT.at[p], GH.at[p])
        ghost_tiles(old + 2.0 * change, GH.at[p])
        substep(A.at[p], B.at[p], HZ.at[p], HX.at[p], HY.at[p], HT.at[p], KY.at[p], KX.at[p], RT.at[p], GH.at[p])
        ghost_tiles(old + 3.0 * change, GH.at[p])
        substep(B.at[p], A.at[p], HZ.at[p], HX.at[p], HY.at[p], HT.at[p], KY.at[p], KX.at[p], RT.at[p], GH.at[p])
        value = patch_average(A.at[p], W)
        for s in range(3):
            AVG[p, s] = value[s * 8 : s * 8 + 8]
        return carry

    def write_patch(p, carry):
        for t in range(TILES):
            for s in range(3):
                for j in range(RATIO):
                    result[p, s, t, pl.ds(j, 8, stride=4), :] = A[p, s, j + 1, :, pl.ds(t * 128, 128)]
        for copy in store_patch(result, fine_out, p, sem_out):
            copy.start()
        return carry

    def two_patches(pair, carry):
        lax.fori_loop(2 * pair, 2 * pair + 2, one_patch, 0)
        for s in range(3):
            both = jnp.where(lanes() < 64, AVG[2 * pair, s], rot(AVG[2 * pair + 1, s], 64))
            PAIR[pair, s] = both
            RECVA[pair, 0, s] = both

        for o in range(1, N_AF):
            average_copy(pair, o).start()
        return carry

    lax.fori_loop(0, 2, two_patches, 0)
    lax.fori_loop(0, SLOT_DEV, write_patch, 0)
    down.wait()
    up.wait()
    lane = lanes()
    change_low = edge_change(E[0], E[2], (col > 0).astype(jnp.float32))
    change_high = edge_change(E[1], E[3], (col < N_COL - 1).astype(jnp.float32))
    for s in range(3):
        for x in range(16):
            i = s * 16 + x
            N[s, x, :, 0:128] += jnp.where(lane == 0, rot(change_low, -i), 0.0)
            N[s, x, :, 128:256] += jnp.where(lane == 127, rot(change_high, 127 - i), 0.0)
    place_tables(cover, PAIR_AT, FROM_AT, ODD, COVERED)
    wait_messages(RECV0, exchange.at[0], exchange.at[1], False)
    wait_messages(RECV1, exchange.at[2], exchange.at[3], False)

    for pair in range(2):
        wait_messages(RECVA.at[pair], averaged.at[0, pair], averaged.at[1, pair], False)
        wait_messages(RECVA.at[pair], averaged.at[0, pair], averaged.at[1, pair], True)
    place_averages(PAIR_AT, FROM_AT, ODD, COVERED, RECVA, N, T)
    for s in range(3):
        coarse_out[s] = jnp.transpose(T[s], (1, 0, 2))

    def end_store(p, carry):
        for copy in store_patch(result, fine_out, p, sem_out):
            copy.wait()
        return carry

    lax.fori_loop(0, SLOT_DEV, end_store, 0)


def per_device(
    coarse_state, coarse_kappa, coarse_rate, fine_state, fine_kappa, fine_rate, boxes, cover
):
    f32 = jnp.float32
    hbm = pl.BlockSpec(memory_space=pl.ANY)
    vmem = pl.BlockSpec(memory_space=pltpu.VMEM)
    D = SLOT_DEV
    message = pltpu.VMEM((N_AF, 3, 8, 128), f32)
    table = pltpu.SMEM((128,), jnp.int32)
    sems = pltpu.SemaphoreType.DMA
    return pl.pallas_call(
        kernel,
        out_shape=(
            pltpu.VMEM((3, NZC, 16, 256), f32),
            pltpu.VMEM((D, 3, FZ, FXY), f32),
        ),
        in_specs=[hbm] * 8,
        out_specs=(vmem, vmem),
        scratch_shapes=[
            pltpu.SMEM((2, 512), jnp.int32),
            pltpu.SMEM((64, 128), jnp.int32),
            table,
            table,
            table,
            table,
            table,
            pltpu.VMEM((5, 8, 128), f32),
            pltpu.VMEM((4, 8, 128), f32),
            pltpu.VMEM((FXY, 128), jnp.bfloat16),
            pltpu.VMEM((5, 8, 16, 256), f32),
            pltpu.VMEM((5, 18, 8, 256), f32),
            pltpu.VMEM((3, 16, 8, 256), f32),
            pltpu.VMEM((3, 16, 8, 256), f32),
            pltpu.VMEM((4, 8, 128), f32),
            pltpu.VMEM((64, 8, 128), f32),
            message,
            message,
            message,
            message,
            pltpu.VMEM((2, 3, 8, 128), f32),
            pltpu.VMEM((D, 3, 8, 128), f32),
            pltpu.VMEM((2, N_AF, 3, 8, 128), f32),
            pltpu.VMEM((D, 3, TILES, FZ, 128), f32),
            pltpu.VMEM((D, TILES, FZ, 128), f32),
            pltpu.VMEM((D, TILES, FZ, 128), f32),
            pltpu.VMEM((D, 3, TILES, FZ, 128), f32),
            pltpu.VMEM((D, 3, RATIO + 2, 8, FXY), f32),
            pltpu.VMEM((D, 3, RATIO + 2, 8, FXY), f32),
            pltpu.VMEM((D, RATIO + 1, 8, FXY), f32),
            pltpu.VMEM((D, RATIO, 2, 8, FXY), f32),
            pltpu.VMEM((D, RATIO, 2, 8, FXY), f32),
            pltpu.VMEM((D, RATIO, 8, FXY), f32),
            pltpu.VMEM((D, RATIO, 8, FXY), f32),
            pltpu.VMEM((D, RATIO, 2, 8, 128), f32),
            pltpu.VMEM((D, RATIO, 8, FXY), f32),
            pltpu.VMEM((D, 3, TILES + 1, 8, 128), f32),
            pltpu.VMEM((2, D, 8, 128), f32),
            sems((5,)),
            sems((2, 4)),
            sems((4,)),
            sems((2, 2)),
            sems((D,)),
            sems((D,)),
        ],
        compiler_params=pltpu.CompilerParams(
            collective_id=0, has_side_effects=True, vmem_limit_bytes=60 * 1024 * 1024
        ),
    )(
        *[
            pltpu.with_memory_space_constraint(x, pltpu.HBM)
            for x in (coarse_state, coarse_kappa, coarse_rate, fine_state, fine_kappa, fine_rate, boxes.T, cover)
        ]
    )


def solution(mesh):
    return jax.shard_map(
        per_device,
        mesh=mesh,
        in_specs=(
            P(None, None, "af", "col"),
            P(None, "af", "col"),
            P(None, "af", "col"),
            P(("col", "af"), None, None, None),
            P(("col", "af"), None, None),
            P(("col", "af"), None, None),
            P(),
            P(),
        ),
        out_specs=(P(None, None, "af", "col"), P(("col", "af"), None, None, None)),
        check_vma=False,
    )
```
